32 devices in a mesh: rows: 8 (over y, x, core), reg: 4 (over z).
Axes of the slice: x: 2, y: 2, z: 4, core: 2. Of those that a mesh axis runs over, the one named last changes fastest.
Arguments:
- snapshots: bfloat16 [65536, 1024], P('rows', 'reg'), may hold values from -6 to 6
- rates: bfloat16 [65536, 1024], P('rows', 'reg'), may hold values from -6 to 6
- basis: bfloat16 [65536, 128], P('rows'), may hold values from -0.0234375 to 0.0234375
Outputs:
- gram: float32 [8384, 8384], P('rows', 'reg')
- rhs: float32 [8384, 128], P('rows')
The draws below stay inside these ranges and needn't reach their ends.
All inputs are finite; a program needn't handle non-finite values.
Results may differ from the reference program's by a relative error of at most 0.0042.
Values may be sent and summed in bfloat16 or wider, within the bound.
No kernel may reach another device: no remote copies, remote signals or barrier semaphores. Data moves between devices by JAX's collectives and lax.ppermute only.
A program may use at most 128 MiB of HBM per device.

```python
import jax
import jax.numpy as jnp
import numpy as np

R = 128
NROWS = 65536
NT = 1024


def level_of(own_key, shape, pieces, low, high):
    level = 1.0
    for axis_at, blocks in pieces:
        steps = jax.random.uniform(jax.random.fold_in(jax.random.fold_in(own_key, 6), axis_at), (blocks,), jnp.float32, low / len(pieces), high / len(pieces))
        level = level * jnp.repeat(jnp.exp(steps), shape[axis_at] // blocks).reshape((-1,) + (1,) * (len(shape) - 1 - axis_at))
    return level


def bell_draw(own_key, extent, scale, most, cuts=(), dtype=jnp.bfloat16):
    level = level_of(own_key, extent, cuts, -0.22, 0.18) if cuts else 1.0
    drawn = jax.random.normal(own_key, extent, jnp.float32) * scale * level
    return jnp.minimum(jnp.maximum(drawn, -most), most).astype(dtype)


def setup_inputs(seed: int = 0) -> dict:
    key_of = jax.random.split(jax.random.key(seed), 4)
    snapshots = bell_draw(key_of[0], (NROWS, NT), 1.0, 6.0, ((0, 8), (1, 4)))
    rates = bell_draw(key_of[1], (NROWS, NT), 1.0, 6.0, ((0, 8), (1, 4)))
    basis = bell_draw(key_of[2], (NROWS, R), NROWS ** -0.5, 0.0234375, ((0, 8),))
    return dict(snapshots=snapshots, rates=rates, basis=basis)


def make_features(states):
    upper_i, upper_j = np.triu_indices(states.shape[0])
    quad = jnp.take(states, upper_i, axis=0) * jnp.take(states, upper_j, axis=0)
    return jnp.concatenate([states, quad], axis=0).astype(jnp.bfloat16)


def reference(snapshots, rates, basis):
    states = jnp.dot(basis.T, snapshots, preferred_element_type=jnp.float32)
    moments = jnp.dot(basis.T, rates, preferred_element_type=jnp.float32).astype(jnp.bfloat16)
    features = make_features(states)
    gram = jnp.dot(features, features.T, preferred_element_type=jnp.float32) / float(NT)
    rhs = jnp.dot(features, moments.T, preferred_element_type=jnp.float32) / float(NT)
    return gram, rhs
```

```python
import functools

import jax
import jax.numpy as jnp
from jax import lax
from jax.experimental import pallas as pl
from jax.experimental.pallas import tpu as pltpu
from jax.sharding import PartitionSpec as P

TILE = 256
MIB = 1 << 20


def round_up(value, step):
    return (value + step - 1) // step * step


def partners(size):
    if size & (size - 1) == 0:
        return [[(i, i ^ k) for i in range(size)] for k in range(1, size)]
    return [[(i, (i + k) % size) for i in range(size)] for k in range(1, size)]


def project_kernel(place, basis_ref, snap_ref, rate_ref, keep_ref, send_ref, acc):
    step = pl.program_id(0)
    half = acc.shape[1] // 2
    contract = (((0,), (0,)), ((), ()))
    left = basis_ref[...]
    part_states = lax.dot_general(left, snap_ref[...], contract, preferred_element_type=jnp.float32)
    part_rates = lax.dot_general(left, rate_ref[...], contract, preferred_element_type=jnp.float32)

    @pl.when(step == 0)
    def _():
        acc[0] = part_states
        acc[1] = part_rates

    @pl.when(step > 0)
    def _():
        acc[0] += part_states
        acc[1] += part_rates

    @pl.when(step == pl.num_programs(0) - 1)
    def _():
        mine = pl.multiple_of(place[0] * half, half)
        other = pl.multiple_of(half - place[0] * half, half)
        for part in range(2):
            keep_ref[part] = acc[part, pl.ds(mine, half), :]
            send_ref[part] = acc[part, pl.ds(other, half), :]


def project(place, basis, snapshots, rates):
    rows, rank = basis.shape
    times = snapshots.shape[1]
    chunk = rows
    while chunk > 1024 and chunk % 2 == 0:
        chunk //= 2
    out = jax.ShapeDtypeStruct((2, rank // 2, times), jnp.float32)
    return pl.pallas_call(
        project_kernel,
        grid_spec=pltpu.PrefetchScalarGridSpec(
            num_scalar_prefetch=1,
            grid=(rows // chunk,),
            in_specs=[
                pl.BlockSpec((chunk, rank), lambda i, s: (i, 0)),
                pl.BlockSpec((chunk, times), lambda i, s: (i, 0)),
                pl.BlockSpec((chunk, times), lambda i, s: (i, 0)),
            ],
            out_specs=[pl.BlockSpec((2, rank // 2, times), lambda i, s: (0, 0, 0))] * 2,
            scratch_shapes=[pltpu.VMEM((2, rank, times), jnp.float32)],
        ),
        out_shape=[out, out],
        compiler_params=pltpu.CompilerParams(vmem_limit_bytes=24 * MIB),
        cost_estimate=pl.CostEstimate(
            flops=4 * rows * rank * times, bytes_accessed=2 * rows * (rank + 2 * times), transcendentals=0
        ),
        name="project",
    )(place, basis, snapshots, rates)


def combine_kernel(*refs):
    out_ref = refs[-1]
    total = refs[0][...]
    for ref in refs[1:-1]:
        total = total + ref[...]
    half = total.shape[1]
    states = total[0]
    high = states.astype(jnp.bfloat16)
    out_ref[0:half] = high
    out_ref[half : 2 * half] = (states - high.astype(jnp.float32)).astype(jnp.bfloat16)
    out_ref[2 * half :] = total[1].astype(jnp.bfloat16)


def combine(parts):
    _, half, times = parts[0].shape
    return pl.pallas_call(
        combine_kernel,
        out_shape=jax.ShapeDtypeStruct((3 * half, times), jnp.bfloat16),
        name="combine",
    )(*parts)


def feature_rows(first, count, rank, states):
    shape = (count, rank)
    feature = first + lax.broadcasted_iota(jnp.int32, shape, 0)
    lane = lax.broadcasted_iota(jnp.int32, shape, 1)
    run_start = rank + lane * rank - (lane * (lane - 1)) // 2
    run_end = run_start + rank - lane
    in_run = (feature >= run_start) & (feature < run_end)
    shift = jnp.sum(jnp.where(in_run, run_start - lane, 0), axis=1, keepdims=True)
    left = in_run.astype(jnp.float32).astype(jnp.bfloat16)
    right = (lane == feature - shift).astype(jnp.float32).astype(jnp.bfloat16)
    pick = functools.partial(jnp.dot, preferred_element_type=jnp.float32)
    left_rows = pick(jnp.concatenate([left, left], axis=1), states)
    right_rows = pick(jnp.concatenate([right, right], axis=1), states)
    linear = (feature[:, :1] < rank).astype(jnp.float32)
    return ((left_rows + linear) * right_rows).astype(jnp.bfloat16)


def gram_kernel(slabs, total_time, place, *refs):
    own, other = refs[:slabs], refs[slabs : 2 * slabs]
    gram_ref, rhs_ref, states, moments, row_feat, col_feat = refs[2 * slabs :]
    step = pl.program_id(0)
    rank = moments.shape[0]
    half, local = rank // 2, own[0].shape[1]
    row_width = gram_ref.shape[0]
    last = pl.num_programs(0) - 1

    @pl.when(step == 0)
    def _():
        for side, pieces in ((0, own), (1, other)):
            at = (place[0] + side) % 2 * half
            for k, piece in enumerate(pieces):
                columns = slice(k * local, (k + 1) * local)
                states[pl.ds(pl.multiple_of(at, half), half), columns] = piece[0:half]
                states[pl.ds(pl.multiple_of(rank + at, half), half), columns] = piece[half : 2 * half]
                moments[pl.ds(pl.multiple_of(at, half), half), columns] = piece[2 * half :]
        for low in range(0, row_feat.shape[0], TILE):
            count = min(TILE, row_feat.shape[0] - low)
            row_feat[low : low + count] = feature_rows(place[1] + low, count, rank, states[...])

    col_feat[...] = feature_rows(place[2] + step * TILE, TILE, rank, states[...])

    @pl.when(step == last)
    def _():
        col_feat[TILE - rank :] = moments[...]

    product = lax.dot_general(
        row_feat[...], col_feat[...], (((1,), (1,)), ((), ())), preferred_element_type=jnp.float32
    )[:row_width]
    product = product / float(total_time)
    gram_ref[...] = product

    @pl.when(step == last)
    def _():
        rhs_ref[...] = product[:, TILE - rank :]


def gram_and_rhs(place, own, other, rank, row_width, col_width):
    slabs = len(own)
    local = own[0].shape[1]
    total_time = slabs * local
    tiles = (col_width + rank + TILE - 1) // TILE
    row_pad = round_up(row_width, 16)
    piece = pl.BlockSpec((3 * rank // 2, local), lambda i, s: (0, 0))
    return pl.pallas_call(
        functools.partial(gram_kernel, slabs, total_time),
        grid_spec=pltpu.PrefetchScalarGridSpec(
            num_scalar_prefetch=1,
            grid=(tiles,),
            in_specs=[piece] * (2 * slabs),
            out_specs=[
                pl.BlockSpec((row_width, TILE), lambda i, s: (0, i)),
                pl.BlockSpec((row_width, rank), lambda i, s: (0, 0)),
            ],
            scratch_shapes=[
                pltpu.VMEM((2 * rank, total_time), jnp.bfloat16),
                pltpu.VMEM((rank, total_time), jnp.bfloat16),
                pltpu.VMEM((row_pad, total_time), jnp.bfloat16),
                pltpu.VMEM((TILE, total_time), jnp.bfloat16),
            ],
        ),
        out_shape=[
            jax.ShapeDtypeStruct((row_width, col_width), jnp.float32),
            jax.ShapeDtypeStruct((row_width, rank), jnp.float32),
        ],
        compiler_params=pltpu.CompilerParams(vmem_limit_bytes=40 * MIB),
        cost_estimate=pl.CostEstimate(
            flops=2 * row_width * (col_width + rank) * total_time,
            bytes_accessed=4 * row_width * (col_width + rank),
            transcendentals=0,
        ),
        name="gram",
    )(place, *own, *other)


def per_device(snapshots, rates, basis):
    rank = basis.shape[1]
    width = rank + rank * (rank + 1) // 2
    size_rows, size_reg = lax.axis_size("rows"), lax.axis_size("reg")
    row_width, col_width = width // size_rows, width // size_reg
    row_at, reg_at = lax.axis_index("rows"), lax.axis_index("reg")
    place = jnp.stack([row_at % 2, row_at * row_width, reg_at * col_width]).astype(jnp.int32)
    swap = [(i, i ^ 1) for i in range(size_rows)]
    keep, send = project(place, basis, snapshots, rates)
    chip = keep + lax.ppermute(send, "rows", swap)
    plane = [[(2 * a + c, 2 * b + c) for a, b in perm for c in range(2)] for perm in partners(size_rows // 2)]
    mine = combine([chip] + [lax.ppermute(chip, "rows", perm) for perm in plane])
    own = [mine] + [lax.ppermute(mine, "reg", perm) for perm in partners(size_reg)]
    other = [lax.ppermute(piece, "rows", swap) for piece in own]
    return tuple(gram_and_rhs(place, own, other, rank, row_width, col_width))


def solution(mesh):
    return jax.shard_map(
        per_device,
        mesh=mesh,
        in_specs=(P("rows", "reg"), P("rows", "reg"), P("rows", None)),
        out_specs=(P("rows", "reg"), P("rows", None)),
        check_vma=False,
    )
```

```python
import functools

import jax
import jax.numpy as jnp
from jax import lax
from jax.experimental import pallas as pl
from jax.experimental.pallas import tpu as pltpu
from jax.sharding import PartitionSpec as P

TILE = 256
EARLY = 2
BLOCK = 272
CHUNKS = 8
MIB = 1 << 20


def round_up(value, step):
    return (value + step - 1) // step * step


def partners(size):
    if size & (size - 1) == 0:
        return [[(i, i ^ k) for i in range(size)] for k in range(1, size)]
    return [[(i, (i + k) % size) for i in range(size)] for k in range(1, size)]


WHOLE = pl.BlockSpec(memory_space=pltpu.VMEM)
ANYWHERE = pl.BlockSpec(memory_space=pl.ANY)
SCALARS = pl.BlockSpec(memory_space=pltpu.SMEM)


def in_hbm(array):
    return pltpu.with_memory_space_constraint(array, pltpu.HBM)


def in_vmem(array):
    return pltpu.with_memory_space_constraint(array, pltpu.VMEM)


def project_kernel(chunks, basis_hbm, snap_hbm, rate_hbm, keep_ref, send_ref, basis, snap, rate, acc, sems):
    rows = basis.shape[0] // chunks
    half = acc.shape[1] // 2
    copies = []
    for c in range(chunks):
        part = pl.ds(c * rows, rows)
        copies.append(
            [
                pltpu.make_async_copy(source.at[part], target.at[part], sems.at[k, c])
                for k, (source, target) in enumerate(((basis_hbm, basis), (snap_hbm, snap), (rate_hbm, rate)))
            ]
        )
        for copy in copies[-1]:
            copy.start()
    for c in range(chunks):
        for copy in copies[c]:
            copy.wait()
        part = pl.ds(c * rows, rows)
        left = basis[part, :].T
        for k, array in enumerate((snap, rate)):
            product = jnp.dot(left, array[part, :], preferred_element_type=jnp.float32)
            if c == 0:
                acc[k] = product
            else:
                acc[k] += product
    core = lax.axis_index("rows") % 2
    mine = pl.multiple_of(core * half, half)
    other = pl.multiple_of(half - core * half, half)
    for k in range(2):
        keep_ref[k * half : (k + 1) * half] = acc[k, pl.ds(mine, half), :]
        send_ref[k * half : (k + 1) * half] = acc[k, pl.ds(other, half), :]


def project(basis, snapshots, rates):
    rows, rank = basis.shape
    times = snapshots.shape[1]
    chunks = CHUNKS if rows % (16 * CHUNKS) == 0 else 1
    out = pltpu.VMEM((rank, times), jnp.float32)
    return pl.pallas_call(
        functools.partial(project_kernel, chunks),
        in_specs=[ANYWHERE] * 3,
        out_specs=[WHOLE, WHOLE],
        out_shape=[out, out],
        scratch_shapes=[
            pltpu.VMEM((rows, rank), jnp.bfloat16),
            pltpu.VMEM((rows, times), jnp.bfloat16),
            pltpu.VMEM((rows, times), jnp.bfloat16),
            pltpu.VMEM((2, rank, times), jnp.float32),
            pltpu.SemaphoreType.DMA((3, chunks)),
        ],
        compiler_params=pltpu.CompilerParams(vmem_limit_bytes=24 * MIB),
        cost_estimate=pl.CostEstimate(
            flops=4 * rows * rank * times, bytes_accessed=2 * rows * (rank + 2 * times), transcendentals=0
        ),
        name="project",
    )(in_hbm(basis), in_hbm(snapshots), in_hbm(rates))


def feature_rows(first, count, rank, states):
    shape = (count, rank)
    feature = first + lax.broadcasted_iota(jnp.int32, shape, 0)
    lane = lax.broadcasted_iota(jnp.int32, shape, 1)
    run_start = rank + lane * rank - (lane * (lane - 1)) // 2
    run_end = run_start + rank - lane
    in_run = (feature >= run_start) & (feature < run_end)
    shift = jnp.sum(jnp.where(in_run, run_start - lane, 0), axis=1, keepdims=True)
    left = in_run.astype(jnp.float32).astype(jnp.bfloat16)
    right = (lane == feature - shift).astype(jnp.float32).astype(jnp.bfloat16)
    pick = functools.partial(jnp.dot, preferred_element_type=jnp.float32)
    left_rows = pick(jnp.concatenate([left, left], axis=1), states)
    right_rows = pick(jnp.concatenate([right, right], axis=1), states)
    linear = (feature[:, :1] < rank).astype(jnp.float32)
    return ((left_rows + linear) * right_rows).astype(jnp.bfloat16)


def column_features(place, pieces, states, col_feat):
    rank = states.shape[0] // 2
    half, local = rank // 2, pieces[0].shape[1]
    end = col_feat.shape[0] - rank
    for k in range(0, len(pieces), 2):
        columns = slice(k // 2 * local, (k // 2 + 1) * local)
        for side in range(2):
            piece = pieces[k + side]
            at = pl.multiple_of((place[0] + side) % 2 * half, half)
            states[pl.ds(at, half), columns] = piece[0:half]
            states[pl.ds(pl.multiple_of(rank + at, half), half), columns] = piece[half : 2 * half]
            col_feat[pl.ds(pl.multiple_of(end + at, half), half), columns] = piece[2 * half :]
    for low in range(0, end, 3 * TILE):
        count = min(3 * TILE, end - low)
        col_feat[low : low + count] = feature_rows(place[2] + low, count, rank, states[...])


def block_product(place, states, col_feat):
    rank = states.shape[0] // 2
    rows = feature_rows(place[1] + pl.program_id(0) * BLOCK, BLOCK, rank, states[...])
    return lax.dot_general(rows, col_feat[...], (((1,), (1,)), ((), ())), preferred_element_type=jnp.float32)


def early_kernel(count, place, *refs):
    pieces, (acc_ref, token_ref, states, col_feat) = refs[:count], refs[count:]
    step = pl.program_id(0)

    @pl.when(step == 0)
    def _():
        token_ref[...] = jnp.zeros_like(token_ref)
        column_features(place, pieces, states, col_feat)

    acc_ref[pl.ds(pl.multiple_of(step * BLOCK, BLOCK), BLOCK), :] = block_product(place, states, col_feat)


def late_kernel(count, total_time, place, *refs):
    pieces, (acc_ref, gram_ref, rhs_ref, states, col_feat) = refs[:count], refs[count:]
    step = pl.program_id(0)
    rank = rhs_ref.shape[1]

    @pl.when(step == 0)
    def _():
        column_features(place, pieces, states, col_feat)

    earlier = acc_ref[pl.ds(pl.multiple_of(step * BLOCK, BLOCK), BLOCK), :]
    product = (earlier + block_product(place, states, col_feat)) / float(total_time)
    gram_ref[...] = product[:, : gram_ref.shape[1]]
    rhs_ref[...] = product[:, product.shape[1] - rank :]


def gram_call(kernel, name, place, pieces, extra, out_specs, out_shape, rank, row_width, col_width):
    slabs, local = len(pieces) // 2, pieces[0].shape[1]
    col_pad = round_up(col_width + rank, TILE)
    operands = [*map(in_vmem, pieces), *map(in_vmem, extra)]
    return pl.pallas_call(
        kernel,
        grid=(-(-row_width // BLOCK),),
        in_specs=[SCALARS] + [WHOLE] * len(operands),
        out_specs=out_specs,
        out_shape=out_shape,
        scratch_shapes=[
            pltpu.VMEM((2 * rank, slabs * local), jnp.bfloat16),
            pltpu.VMEM((col_pad, slabs * local), jnp.bfloat16),
        ],
        compiler_params=pltpu.CompilerParams(vmem_limit_bytes=32 * MIB),
        cost_estimate=pl.CostEstimate(
            flops=0,
            bytes_accessed=0,
            transcendentals=0,
        ),
        name=name,
    )(place, *operands)


def per_device(snapshots, rates, basis):
    rank = basis.shape[1]
    width = rank + rank * (rank + 1) // 2
    size_rows, size_reg = lax.axis_size("rows"), lax.axis_size("reg")
    row_width, col_width = width // size_rows, width // size_reg
    row_at, reg_at = lax.axis_index("rows"), lax.axis_index("reg")
    total_time = snapshots.shape[1] * size_reg
    place = jnp.stack([row_at % 2, row_at * row_width, reg_at * col_width]).astype(jnp.int32)
    swap = [(i, i ^ 1) for i in range(size_rows)]
    keep, send = project(basis, snapshots, rates)
    chip = keep + lax.ppermute(send, "rows", swap)
    plane = [[(2 * a + c, 2 * b + c) for a, b in perm for c in range(2)] for perm in partners(size_rows // 2)]
    total = chip
    for perm in plane:
        total = total + lax.ppermute(chip, "rows", perm)
    states, moments = total[: rank // 2], total[rank // 2 :]
    high = lax.reduce_precision(states, 8, 7)
    mine = jnp.concatenate([high, states - high, moments]).astype(jnp.bfloat16)
    own = [mine] + [lax.ppermute(mine, "reg", perm) for perm in partners(size_reg)]
    shape = (rank, row_width, col_width)

    early, late = own[:EARLY], own[EARLY:]
    pieces = [half for piece in early for half in (piece, lax.ppermute(piece, "rows", swap))]
    row_pad, col_pad = round_up(row_width, BLOCK), round_up(col_width + rank, TILE)
    earlier, token = gram_call(
        functools.partial(early_kernel, len(pieces)), "early", place, pieces, [], [WHOLE, WHOLE],
        [pltpu.VMEM((row_pad, col_pad), jnp.float32), pltpu.VMEM(mine.shape, jnp.bfloat16)], *shape,
    )
    late = [piece + token for piece in late]
    pieces = [half for piece in late for half in (piece, lax.ppermute(piece, "rows", swap))]
    return tuple(
        gram_call(
            functools.partial(late_kernel, len(pieces), total_time), "late", place, pieces, [earlier],
            [pl.BlockSpec((BLOCK, col_width), lambda i: (i, 0)), pl.BlockSpec((BLOCK, rank), lambda i: (i, 0))],
            [jax.ShapeDtypeStruct((row_width, n), jnp.float32) for n in (col_width, rank)], *shape,
        )
    )


def solution(mesh):
    return jax.shard_map(
        per_device,
        mesh=mesh,
        in_specs=(P("rows", "reg"), P("rows", "reg"), P("rows", None)),
        out_specs=(P("rows", "reg"), P("rows", None)),
        check_vma=False,
    )
```

```python
import functools

import jax
import jax.numpy as jnp
from jax import lax
from jax.experimental import pallas as pl
from jax.experimental.pallas import tpu as pltpu
from jax.sharding import PartitionSpec as P

TILE = 256
ROWS = 352
COLS = 768
CHUNKS = 8
MIB = 1 << 20


def round_up(value, step):
    return (value + step - 1) // step * step


def partners(size):
    if size & (size - 1) == 0:
        return [[(i, i ^ k) for i in range(size)] for k in range(1, size)]
    return [[(i, (i + k) % size) for i in range(size)] for k in range(1, size)]


WHOLE = pl.BlockSpec(memory_space=pltpu.VMEM)
ANYWHERE = pl.BlockSpec(memory_space=pl.ANY)
LONG = pl.CostEstimate(flops=20_000_000_000, bytes_accessed=0, transcendentals=0)
FREE = pl.CostEstimate(flops=0, bytes_accessed=0, transcendentals=0)


def in_hbm(array):
    return pltpu.with_memory_space_constraint(array, pltpu.HBM)


def in_vmem(array):
    return pltpu.with_memory_space_constraint(array, pltpu.VMEM)


def project_kernel(chunks, basis_hbm, snap_hbm, rate_hbm, keep_ref, send_ref, basis, snap, rate, acc, sems):
    rows = basis.shape[0] // chunks
    copies = []
    for c in range(chunks):
        part = pl.ds(c * rows, rows)
        copies.append(
            [
                pltpu.make_async_copy(source.at[part], target.at[part], sems.at[k, c])
                for k, (source, target) in enumerate(((basis_hbm, basis), (snap_hbm, snap), (rate_hbm, rate)))
            ]
        )
        for copy in copies[-1]:
            copy.start()
    for c in range(chunks):
        for copy in copies[c]:
            copy.wait()
        part = pl.ds(c * rows, rows)
        left = basis[part, :].T
        for k, array in enumerate((snap, rate)):
            product = jnp.dot(left, array[part, :], preferred_element_type=jnp.float32)
            if c == 0:
                acc[k] = product
            else:
                acc[k] += product
    rank, half = acc.shape[1], acc.shape[2] // 2
    core = lax.axis_index("rows") % 2
    mine = pl.multiple_of(core * half, half)
    other = pl.multiple_of(half - core * half, half)
    for k in range(2):
        keep_ref[k * rank : (k + 1) * rank] = acc[k, :, pl.ds(mine, half)]
        send_ref[k * rank : (k + 1) * rank] = acc[k, :, pl.ds(other, half)]


def project(basis, snapshots, rates):
    rows, rank = basis.shape
    times = snapshots.shape[1]
    chunks = CHUNKS if rows % (16 * CHUNKS) == 0 else 1
    out = pltpu.VMEM((2 * rank, times // 2), jnp.float32)
    return pl.pallas_call(
        functools.partial(project_kernel, chunks),
        in_specs=[ANYWHERE] * 3,
        out_specs=[WHOLE, WHOLE],
        out_shape=[out, out],
        scratch_shapes=[
            pltpu.VMEM((rows, rank), jnp.bfloat16),
            pltpu.VMEM((rows, times), jnp.bfloat16),
            pltpu.VMEM((rows, times), jnp.bfloat16),
            pltpu.VMEM((2, rank, times), jnp.float32),
            pltpu.SemaphoreType.DMA((3, chunks)),
        ],
        compiler_params=pltpu.CompilerParams(vmem_limit_bytes=24 * MIB),
        cost_estimate=pl.CostEstimate(
            flops=4 * rows * rank * times, bytes_accessed=2 * rows * (rank + 2 * times), transcendentals=0
        ),
        name="project",
    )(in_hbm(basis), in_hbm(snapshots), in_hbm(rates))


def feature_rows(first, count, rank, states):
    shape = (count, rank)
    feature = first + lax.broadcasted_iota(jnp.int32, shape, 0)
    lane = lax.broadcasted_iota(jnp.int32, shape, 1)
    run_start = rank + lane * rank - (lane * (lane - 1)) // 2
    run_end = run_start + rank - lane
    in_run = (feature >= run_start) & (feature < run_end)
    shift = jnp.sum(jnp.where(in_run, run_start - lane, 0), axis=1, keepdims=True)
    left = in_run.astype(jnp.float32).astype(jnp.bfloat16)
    right = (lane == feature - shift).astype(jnp.float32).astype(jnp.bfloat16)
    pick = functools.partial(jnp.dot, preferred_element_type=jnp.float32)
    left_rows = pick(jnp.concatenate([left, left], axis=1), states)
    right_rows = pick(jnp.concatenate([right, right], axis=1), states)
    linear = (feature[:, :1] < rank).astype(jnp.float32)
    return ((left_rows + linear) * right_rows).astype(jnp.bfloat16)


def lay_out(pieces, states, moments):
    rank, at = moments.shape[0], 0
    for piece in pieces:
        for low in range(0, piece.shape[0], 3 * rank):
            columns = slice(at, at + piece.shape[1])
            states[:, columns] = piece[low : low + 2 * rank]
            moments[:, columns] = piece[low + 2 * rank : low + 3 * rank]
            at += piece.shape[1]


def spans(total, most):
    return [(low, min(most, total - low)) for low in range(0, total, most)]


def fill_rows(row_width, states, row_feat, columns):
    rank, first = states.shape[0] // 2, lax.axis_index("rows") * row_width
    for low, size in spans(row_feat.shape[0], ROWS):
        row_feat[low : low + size, columns] = feature_rows(first + low, size, rank, states[...])


def fill_columns(col_width, states, moments, col_feat, left, right, columns):
    rank, first = moments.shape[0], lax.axis_index("reg") * col_width
    end = min(right, col_feat.shape[0] - rank)
    col_feat[left:end, columns] = feature_rows(first + left, end - left, rank, states[...])
    if end < right:
        col_feat[end:right, columns] = moments[...]


def prepare_kernel(count, row_width, col_width, *refs):
    pieces, (row_feat, col_feat, *zero, states, moments) = refs[:count], refs[count:]
    for ref in zero:
        ref[...] = jnp.zeros_like(ref)
    lay_out(pieces, states, moments)
    fill_rows(row_width, states, row_feat, slice(None))
    for left, width in spans(col_feat.shape[0], COLS):
        fill_columns(col_width, states, moments, col_feat, left, left + width, slice(None))


def prepare(pieces, waiting, cost, rank, row_width, col_width):
    times = sum(piece.size for piece in pieces) // (3 * rank)
    row_pad, col_pad = round_up(row_width, 16), round_up(col_width + rank, TILE)
    return pl.pallas_call(
        functools.partial(prepare_kernel, len(pieces), row_width, col_width),
        in_specs=[WHOLE] * len(pieces),
        out_specs=[WHOLE] * (2 + len(waiting)),
        out_shape=[pltpu.VMEM(shape, jnp.bfloat16) for shape in [(row_pad, times), (col_pad, times), *waiting]],
        scratch_shapes=[pltpu.VMEM((n * rank, times), jnp.bfloat16) for n in (2, 1)],
        compiler_params=pltpu.CompilerParams(vmem_limit_bytes=32 * MIB),
        cost_estimate=cost,
        name="prepare",
    )(*map(in_vmem, pieces))


def sum_kernel(count, held, ready, total_time, row_width, col_width, *refs):
    pieces, refs = refs[:count], refs[count:]
    acc_in, refs = (refs[0], refs[1:]) if held else (None, refs)
    (row_ready, col_ready), refs = (refs[:2], refs[2:]) if ready else ((None, None), refs)
    refs = refs[1:]
    states, moments, row_feat, col_feat = refs[-4:]
    rank = moments.shape[0]
    row_pad, col_pad = row_feat.shape[0], col_feat.shape[0]
    columns = slice(row_feat.shape[1] - states.shape[1], row_feat.shape[1])
    before = slice(0, columns.start)
    lay_out(pieces, states, moments)
    fill_rows(row_width, states, row_feat, columns)
    if ready:
        row_feat[:, before] = row_ready[...]
    copies = []
    for left, width in spans(col_pad, COLS):
        fill_columns(col_width, states, moments, col_feat, left, left + width, columns)
        if ready:
            col_feat[left : left + width, before] = col_ready[left : left + width]
        for low, size in spans(row_pad, ROWS):
            block = lax.dot_general(
                row_feat[low : low + size], col_feat[left : left + width], (((1,), (1,)), ((), ())),
                preferred_element_type=jnp.float32,
            )
            if held:
                block = acc_in[low : low + size, left : left + width] + block
            if total_time is None:
                refs[0][low : low + size, left : left + width] = block
                if left + low == 0:
                    refs[1][...] = jnp.zeros_like(refs[1])
                continue
            gram_hbm, rhs_hbm, gram, rhs, sems = refs[:5]
            block = block / float(total_time)
            rows = pl.ds(low, min(size, row_width - low))
            if left < col_width:
                part = pl.ds(left, min(width, col_width - left))
                gram[rows, part] = block[: rows.size, : part.size]
                copies.append(pltpu.make_async_copy(gram.at[rows, part], gram_hbm.at[rows, part], sems.at[len(copies)]))
                copies[-1].start()
            if left + width == col_pad:
                rhs[rows] = block[: rows.size, width - rank :]
                copies.append(pltpu.make_async_copy(rhs.at[rows], rhs_hbm.at[rows], sems.at[len(copies)]))
                copies[-1].start()
    for copy in copies:
        copy.wait()


def add_up(place, pieces, held, ready, total_time, waiting, rank, row_width, col_width):
    times = sum(piece.size for piece in pieces) // (3 * rank)
    all_times = times + (ready[0].shape[1] if ready else 0)
    row_pad, col_pad = round_up(row_width, 16), round_up(col_width + rank, TILE)
    operands = [*map(in_vmem, pieces), *map(in_vmem, held), *map(in_vmem, ready)]
    operands += [in_vmem(place)]
    scratch = [
        pltpu.VMEM((2 * rank, times), jnp.bfloat16),
        pltpu.VMEM((rank, times), jnp.bfloat16),
        pltpu.VMEM((row_pad, all_times), jnp.bfloat16),
        pltpu.VMEM((col_pad, all_times), jnp.bfloat16),
    ]
    if total_time is None:
        out_specs = [WHOLE, WHOLE]
        out_shape = [pltpu.VMEM((row_pad, col_pad), jnp.float32), pltpu.VMEM(waiting, jnp.bfloat16)]
    else:
        out_specs = [ANYWHERE, ANYWHERE]
        out_shape = [jax.ShapeDtypeStruct((row_width, n), jnp.float32) for n in (col_width, rank)]
        scratch = [
            pltpu.VMEM((row_width, col_width), jnp.float32),
            pltpu.VMEM((row_width, rank), jnp.float32),
            pltpu.SemaphoreType.DMA((len(spans(row_pad, ROWS)) * (len(spans(col_pad, COLS)) + 1),)),
        ] + scratch
    return pl.pallas_call(
        functools.partial(sum_kernel, len(pieces), bool(held), bool(ready), total_time, row_width, col_width),
        in_specs=[WHOLE] * len(operands),
        out_specs=out_specs,
        out_shape=out_shape,
        scratch_shapes=scratch,
        compiler_params=pltpu.CompilerParams(vmem_limit_bytes=32 * MIB),
        cost_estimate=FREE,
        name="add_up_last" if total_time else "add_up",
    )(*operands)


def per_device(snapshots, rates, basis):
    rank = basis.shape[1]
    width = rank + rank * (rank + 1) // 2
    size_rows, size_reg = lax.axis_size("rows"), lax.axis_size("reg")
    row_width, col_width = width // size_rows, width // size_reg
    total_time = snapshots.shape[1] * size_reg
    shape = (rank, row_width, col_width)

    place = jnp.stack([lax.axis_index("rows") * row_width, lax.axis_index("reg") * col_width]).astype(jnp.int32)
    swap = [(i, i ^ 1) for i in range(size_rows)]
    keep, send = project(basis, snapshots, rates)
    chip = keep + lax.ppermute(send, "rows", swap)
    plane = [[(2 * a + c, 2 * b + c) for a, b in perm for c in range(2)] for perm in partners(size_rows // 2)]
    total = chip
    for perm in plane:
        total = total + lax.ppermute(chip, "rows", perm)
    states, moments = total[:rank], total[rank:]
    high = lax.reduce_precision(states, 8, 7)
    mine = jnp.concatenate([high, states - high, moments]).astype(jnp.bfloat16)
    slabs = [mine] + [lax.ppermute(mine, "reg", perm) for perm in partners(size_reg)]

    near, far = slabs[-1:], slabs[-2:0:-1]
    *ready, zero = prepare([mine, lax.ppermute(mine, "rows", swap)], [mine.shape], LONG, *shape)
    near = [slab + zero for slab in near]
    pieces = [half for slab in near for half in (slab, lax.ppermute(slab, "rows", swap))]
    waiting = (len(far) * mine.shape[0], mine.shape[1])
    *held, zero = add_up(place, pieces, [], ready, None, waiting, *shape)
    piece = jnp.concatenate(far) + zero
    other = lax.ppermute(piece, "rows", swap)
    ready = prepare([piece], [], FREE, *shape)
    return tuple(add_up(place, [other], held, ready, total_time, None, *shape))


def solution(mesh):
    return jax.shard_map(
        per_device,
        mesh=mesh,
        in_specs=(P("rows", "reg"), P("rows", "reg"), P("rows", None)),
        out_specs=(P("rows", "reg"), P("rows", None)),
        check_vma=False,
    )
```

```python
import functools

import jax
import jax.numpy as jnp
from jax import lax
from jax.experimental import pallas as pl
from jax.experimental.pallas import tpu as pltpu
from jax.sharding import PartitionSpec as P

TILE = 256
ROWS = 352
COLS = 768
CHUNKS = 8
MIB = 1 << 20


def round_up(value, step):
    return (value + step - 1) // step * step


def partners(size):
    if size & (size - 1) == 0:
        return [[(i, i ^ k) for i in range(size)] for k in range(1, size)]
    return [[(i, (i + k) % size) for i in range(size)] for k in range(1, size)]


WHOLE = pl.BlockSpec(memory_space=pltpu.VMEM)
ANYWHERE = pl.BlockSpec(memory_space=pl.ANY)
LONG = pl.CostEstimate(flops=20_000_000_000, bytes_accessed=0, transcendentals=0)
FREE = pl.CostEstimate(flops=0, bytes_accessed=0, transcendentals=0)


def in_hbm(array):
    return pltpu.with_memory_space_constraint(array, pltpu.HBM)


def in_vmem(array):
    return pltpu.with_memory_space_constraint(array, pltpu.VMEM)


def project_kernel(chunks, basis_hbm, snap_hbm, rate_hbm, keep_ref, send_ref, basis, snap, rate, acc, sems):
    rows = basis.shape[0] // chunks
    copies = []
    for c in range(chunks):
        part = pl.ds(c * rows, rows)
        copies.append(
            [
                pltpu.make_async_copy(source.at[part], target.at[part], sems.at[k, c])
                for k, (source, target) in enumerate(((basis_hbm, basis), (snap_hbm, snap), (rate_hbm, rate)))
            ]
        )
        for copy in copies[-1]:
            copy.start()
    for c in range(chunks):
        for copy in copies[c]:
            copy.wait()
        part = pl.ds(c * rows, rows)
        left = basis[part, :].T
        for k, array in enumerate((snap, rate)):
            product = jnp.dot(left, array[part, :], preferred_element_type=jnp.float32)
            if c == 0:
                acc[k] = product
            else:
                acc[k] += product
    rank, half = acc.shape[1], acc.shape[2] // 2
    core = lax.axis_index("rows") % 2
    mine = pl.multiple_of(core * half, half)
    other = pl.multiple_of(half - core * half, half)
    for k in range(2):
        keep_ref[k * rank : (k + 1) * rank] = acc[k, :, pl.ds(mine, half)]
        send_ref[k * rank : (k + 1) * rank] = acc[k, :, pl.ds(other, half)]


def project(basis, snapshots, rates):
    rows, rank = basis.shape
    times = snapshots.shape[1]
    chunks = CHUNKS if rows % (16 * CHUNKS) == 0 else 1
    out = pltpu.VMEM((2 * rank, times // 2), jnp.float32)
    return pl.pallas_call(
        functools.partial(project_kernel, chunks),
        in_specs=[ANYWHERE] * 3,
        out_specs=[WHOLE, WHOLE],
        out_shape=[out, out],
        scratch_shapes=[
            pltpu.VMEM((rows, rank), jnp.bfloat16),
            pltpu.VMEM((rows, times), jnp.bfloat16),
            pltpu.VMEM((rows, times), jnp.bfloat16),
            pltpu.VMEM((2, rank, times), jnp.float32),
            pltpu.SemaphoreType.DMA((3, chunks)),
        ],
        compiler_params=pltpu.CompilerParams(vmem_limit_bytes=24 * MIB),
        cost_estimate=pl.CostEstimate(
            flops=4 * rows * rank * times, bytes_accessed=2 * rows * (rank + 2 * times), transcendentals=0
        ),
        name="project",
    )(in_hbm(basis), in_hbm(snapshots), in_hbm(rates))


def select_kernel(row_width, col_width, row_pick, col_pick, zero_ref):
    rank = row_pick.shape[1] // 2
    zero_ref[...] = jnp.zeros_like(zero_ref)
    for pick, begin in (
        (row_pick, lax.axis_index("rows") * row_width),
        (col_pick, lax.axis_index("reg") * col_width),
    ):
        for low, count in spans(pick.shape[0], TILE):
            shape = (count, rank)
            feature = begin + low + lax.broadcasted_iota(jnp.int32, shape, 0)
            lane = lax.broadcasted_iota(jnp.int32, shape, 1)
            run_start = rank + lane * rank - (lane * (lane - 1)) // 2
            run_end = run_start + rank - lane
            in_run = (feature >= run_start) & (feature < run_end)
            shift = jnp.sum(jnp.where(in_run, run_start - lane, 0), axis=1, keepdims=True)
            pick[low : low + count, :rank] = in_run.astype(jnp.float32).astype(jnp.bfloat16)
            pick[low : low + count, rank:] = (lane == feature - shift).astype(jnp.float32).astype(jnp.bfloat16)


def select(zero, rank, row_width, col_width):
    row_pad, col_pad = round_up(row_width, 16), round_up(col_width + rank, TILE)
    return pl.pallas_call(
        functools.partial(select_kernel, row_width, col_width),
        out_specs=[WHOLE] * 3,
        out_shape=[
            pltpu.VMEM((row_pad, 2 * rank), jnp.bfloat16),
            pltpu.VMEM((col_pad - rank, 2 * rank), jnp.bfloat16),
            pltpu.VMEM(zero.shape, zero.dtype),
        ],
        compiler_params=pltpu.CompilerParams(vmem_limit_bytes=8 * MIB),
        cost_estimate=LONG,
        name="select",
    )()


def feature_rows(first, pick, states):
    rank = pick.shape[1] // 2
    left, right = pick[:, :rank], pick[:, rank:]
    rows = [
        jnp.dot(jnp.concatenate([one_hot, one_hot], axis=1), states, preferred_element_type=jnp.float32)
        for one_hot in (left, right)
    ]
    feature = first + lax.broadcasted_iota(jnp.int32, (pick.shape[0], 1), 0)
    return ((rows[0] + (feature < rank).astype(jnp.float32)) * rows[1]).astype(jnp.bfloat16)


def lay_out(pieces, states, moments):
    rank, at = moments.shape[0], 0
    for piece in pieces:
        for low in range(0, piece.shape[0], 3 * rank):
            columns = slice(at, at + piece.shape[1])
            states[:, columns] = piece[low : low + 2 * rank]
            moments[:, columns] = piece[low + 2 * rank : low + 3 * rank]
            at += piece.shape[1]


def spans(total, most):
    return [(low, min(most, total - low)) for low in range(0, total, most)]


def fill_rows(row_width, pick, states, row_feat, columns):
    first = lax.axis_index("rows") * row_width
    for low, size in spans(row_feat.shape[0], ROWS):
        row_feat[low : low + size, columns] = feature_rows(first + low, pick[low : low + size], states[...])


def fill_columns(col_width, pick, states, moments, col_feat, left, right, columns):
    first, end = lax.axis_index("reg") * col_width, min(right, pick.shape[0])
    col_feat[left:end, columns] = feature_rows(first + left, pick[left:end], states[...])
    if end < right:
        col_feat[end:right, columns] = moments[...]


def prepare_kernel(count, row_width, col_width, *refs):
    pieces, (row_pick, col_pick, row_feat, col_feat, *zero, states, moments) = refs[:count], refs[count:]
    for ref in zero:
        ref[...] = jnp.zeros_like(ref)
    lay_out(pieces, states, moments)
    fill_rows(row_width, row_pick, states, row_feat, slice(None))
    for left, width in spans(col_feat.shape[0], COLS):
        fill_columns(col_width, col_pick, states, moments, col_feat, left, left + width, slice(None))


def prepare(picks, pieces, waiting, cost, rank, row_width, col_width):
    times = sum(piece.size for piece in pieces) // (3 * rank)
    row_pad, col_pad = round_up(row_width, 16), round_up(col_width + rank, TILE)
    return pl.pallas_call(
        functools.partial(prepare_kernel, len(pieces), row_width, col_width),
        in_specs=[WHOLE] * (len(pieces) + 2),
        out_specs=[WHOLE] * (2 + len(waiting)),
        out_shape=[pltpu.VMEM(shape, jnp.bfloat16) for shape in [(row_pad, times), (col_pad, times), *waiting]],
        scratch_shapes=[pltpu.VMEM((n * rank, times), jnp.bfloat16) for n in (2, 1)],
        compiler_params=pltpu.CompilerParams(vmem_limit_bytes=12 * MIB),
        cost_estimate=cost,
        name="prepare",
    )(*map(in_vmem, pieces), *map(in_vmem, picks))


def sum_kernel(count, extra, held, ready, total_time, row_width, col_width, *refs):
    pieces, refs = refs[:count], refs[count:]
    acc_in, refs = (refs[0], refs[1:]) if held else (None, refs)
    (row_ready, col_ready), refs = (refs[:2], refs[2:]) if ready else ((None, None), refs)
    row_pick, col_pick, *refs = refs[extra:]
    states, moments, row_feat, col_feat = refs[-4:]
    rank = moments.shape[0]
    row_pad, col_pad = row_feat.shape[0], col_feat.shape[0]
    columns = slice(row_feat.shape[1] - states.shape[1], row_feat.shape[1])
    before = slice(0, columns.start)
    lay_out(pieces, states, moments)
    fill_rows(row_width, row_pick, states, row_feat, columns)
    if ready:
        row_feat[:, before] = row_ready[...]
    copies = []
    for left, width in spans(col_pad, COLS):
        fill_columns(col_width, col_pick, states, moments, col_feat, left, left + width, columns)
        if ready:
            col_feat[left : left + width, before] = col_ready[left : left + width]
        for low, size in spans(row_pad, ROWS):
            block = lax.dot_general(
                row_feat[low : low + size], col_feat[left : left + width], (((1,), (1,)), ((), ())),
                preferred_element_type=jnp.float32,
            )
            if held:
                block = acc_in[low : low + size, left : left + width] + block
            if total_time is None:
                refs[0][low : low + size, left : left + width] = block
                if left + low == 0:
                    refs[1][...] = jnp.zeros_like(refs[1])
                continue
            gram_hbm, rhs_hbm, gram, rhs, sems = refs[:5]
            block = block * (1 / total_time) if total_time & (total_time - 1) == 0 else block / float(total_time)
            rows = pl.ds(low, min(size, row_width - low))
            if left < col_width:
                part = pl.ds(left, min(width, col_width - left))
                gram[rows, part] = block[: rows.size, : part.size]
                copies.append(pltpu.make_async_copy(gram.at[rows, part], gram_hbm.at[rows, part], sems.at[len(copies)]))
                copies[-1].start()
            if left + width == col_pad:
                rhs[rows] = block[: rows.size, width - rank :]
                copies.append(pltpu.make_async_copy(rhs.at[rows], rhs_hbm.at[rows], sems.at[len(copies)]))
                copies[-1].start()
    for copy in copies:
        copy.wait()


def add_up(picks, place, pieces, held, ready, total_time, waiting, cost, rank, row_width, col_width):
    times = sum(piece.size for piece in pieces) // (3 * rank)
    all_times = times + (ready[0].shape[1] if ready else 0)
    row_pad, col_pad = round_up(row_width, 16), round_up(col_width + rank, TILE)
    operands = [*map(in_vmem, pieces), *map(in_vmem, held), *map(in_vmem, ready), *map(in_vmem, place), *map(in_vmem, picks)]
    scratch = [
        pltpu.VMEM((2 * rank, times), jnp.bfloat16),
        pltpu.VMEM((rank, times), jnp.bfloat16),
        pltpu.VMEM((row_pad, all_times), jnp.bfloat16),
        pltpu.VMEM((col_pad, all_times), jnp.bfloat16),
    ]
    if total_time is None:
        out_specs = [WHOLE, WHOLE]
        out_shape = [pltpu.VMEM((row_pad, col_pad), jnp.float32), pltpu.VMEM(waiting, jnp.bfloat16)]
    else:
        out_specs = [ANYWHERE, ANYWHERE]
        out_shape = [jax.ShapeDtypeStruct((row_width, n), jnp.float32) for n in (col_width, rank)]
        scratch = [
            pltpu.VMEM((row_width, col_width), jnp.float32),
            pltpu.VMEM((row_width, rank), jnp.float32),
            pltpu.SemaphoreType.DMA((len(spans(row_pad, ROWS)) * (len(spans(col_pad, COLS)) + 1),)),
        ] + scratch
    return pl.pallas_call(
        functools.partial(sum_kernel, len(pieces), len(place), bool(held), bool(ready), total_time, row_width, col_width),
        in_specs=[WHOLE] * len(operands),
        out_specs=out_specs,
        out_shape=out_shape,
        scratch_shapes=scratch,
        compiler_params=pltpu.CompilerParams(vmem_limit_bytes=(24 if total_time else 12) * MIB),
        cost_estimate=cost,
        name="add_up_last" if total_time else "add_up",
    )(*operands)


def per_device(snapshots, rates, basis):
    rank = basis.shape[1]
    width = rank + rank * (rank + 1) // 2
    size_rows, size_reg = lax.axis_size("rows"), lax.axis_size("reg")
    row_width, col_width = width // size_rows, width // size_reg
    total_time = snapshots.shape[1] * size_reg
    shape = (rank, row_width, col_width)

    place = jnp.stack([lax.axis_index("rows") * row_width, lax.axis_index("reg") * col_width]).astype(jnp.int32)
    swap = [(i, i ^ 1) for i in range(size_rows)]
    keep, send = project(basis, snapshots, rates)
    chip = keep + lax.ppermute(send, "rows", swap)
    plane = [[(2 * a + c, 2 * b + c) for a, b in perm for c in range(2)] for perm in partners(size_rows // 2)]
    total = chip
    for perm in plane:
        total = total + lax.ppermute(chip, "rows", perm)
    *picks, zero = select(chip, *shape)
    total = total + zero
    states, moments = total[:rank], total[rank:]
    high = lax.reduce_precision(states, 8, 7)
    mine = jnp.concatenate([high, states - high, moments]).astype(jnp.bfloat16)
    slabs = [mine] + [lax.ppermute(mine, "reg", perm) for perm in partners(size_reg)]

    near, far = slabs[-1], slabs[-2:0:-1]
    waiting = [(n * mine.shape[0], mine.shape[1]) for n in (1, len(far))]
    *held, zero = add_up(picks, [], [mine, lax.ppermute(mine, "rows", swap)], [], [], None, waiting[0], LONG, *shape)
    near = near + zero
    pieces = [near, lax.ppermute(near, "rows", swap)]
    *held, zero = add_up(picks, [place], pieces, held, [], None, waiting[1], FREE, *shape)
    far = jnp.concatenate(far) + zero
    other = lax.ppermute(far, "rows", swap)
    ready = prepare(picks, [far], [], FREE, *shape)
    return tuple(add_up(picks, [place], [other], held, ready, total_time, None, FREE, *shape))


def solution(mesh):
    return jax.shard_map(
        per_device,
        mesh=mesh,
        in_specs=(P("rows", "reg"), P("rows", "reg"), P("rows", None)),
        out_specs=(P("rows", "reg"), P("rows", None)),
        check_vma=False,
    )
```

```python
import functools

import jax
import jax.numpy as jnp
from jax import lax
from jax.experimental import pallas as pl
from jax.experimental.pallas import tpu as pltpu
from jax.sharding import PartitionSpec as P

TILE = 256
ROWS = 352
COLS = 768
CHUNKS = 8
MIB = 1 << 20


def round_up(value, step):
    return (value + step - 1) // step * step


def partners(size):
    if size & (size - 1) == 0:
        return [[(i, i ^ k) for i in range(size)] for k in range(1, size)]
    return [[(i, (i + k) % size) for i in range(size)] for k in range(1, size)]


WHOLE = pl.BlockSpec(memory_space=pltpu.VMEM)
ANYWHERE = pl.BlockSpec(memory_space=pl.ANY)
LONG = pl.CostEstimate(flops=20_000_000_000, bytes_accessed=0, transcendentals=0)
FREE = pl.CostEstimate(flops=0, bytes_accessed=0, transcendentals=0)


def in_hbm(array):
    return pltpu.with_memory_space_constraint(array, pltpu.HBM)


def in_vmem(array):
    return pltpu.with_memory_space_constraint(array, pltpu.VMEM)


def project_kernel(chunks, basis_hbm, snap_hbm, rate_hbm, keep_ref, send_ref, basis, snap, rate, acc, sems):
    rows = basis.shape[0] // chunks
    copies = []
    for c in range(chunks):
        part = pl.ds(c * rows, rows)
        copies.append(
            [
                pltpu.make_async_copy(source.at[part], target.at[part], sems.at[k, c])
                for k, (source, target) in enumerate(((basis_hbm, basis), (snap_hbm, snap), (rate_hbm, rate)))
            ]
        )
        for copy in copies[-1]:
            copy.start()
    for c in range(chunks):
        for copy in copies[c]:
            copy.wait()
        part = pl.ds(c * rows, rows)
        left = basis[part, :].T
        for k, array in enumerate((snap, rate)):
            product = jnp.dot(left, array[part, :], preferred_element_type=jnp.float32)
            if c == 0:
                acc[k] = product
            else:
                acc[k] += product
    rank, half = acc.shape[1], acc.shape[2] // 2
    core = lax.axis_index("rows") % 2
    mine = pl.multiple_of(core * half, half)
    other = pl.multiple_of(half - core * half, half)
    for k in range(2):
        keep_ref[k * rank : (k + 1) * rank] = acc[k, :, pl.ds(mine, half)]
        send_ref[k * rank : (k + 1) * rank] = acc[k, :, pl.ds(other, half)]


def project(basis, snapshots, rates):
    rows, rank = basis.shape
    times = snapshots.shape[1]
    chunks = CHUNKS if rows % (16 * CHUNKS) == 0 else 1
    out = pltpu.VMEM((2 * rank, times // 2), jnp.float32)
    return pl.pallas_call(
        functools.partial(project_kernel, chunks),
        in_specs=[ANYWHERE] * 3,
        out_specs=[WHOLE, WHOLE],
        out_shape=[out, out],
        scratch_shapes=[
            pltpu.VMEM((rows, rank), jnp.bfloat16),
            pltpu.VMEM((rows, times), jnp.bfloat16),
            pltpu.VMEM((rows, times), jnp.bfloat16),
            pltpu.VMEM((2, rank, times), jnp.float32),
            pltpu.SemaphoreType.DMA((3, chunks)),
        ],
        compiler_params=pltpu.CompilerParams(vmem_limit_bytes=24 * MIB),
        cost_estimate=pl.CostEstimate(
            flops=4 * rows * rank * times, bytes_accessed=2 * rows * (rank + 2 * times), transcendentals=0
        ),
        name="project",
    )(in_hbm(basis), in_hbm(snapshots), in_hbm(rates))


def select_kernel(row_width, col_width, row_pick, col_pick, zero_ref):
    rank = row_pick.shape[1] // 2
    zero_ref[...] = jnp.zeros_like(zero_ref)
    for pick, begin in (
        (row_pick, lax.axis_index("rows") * row_width),
        (col_pick, lax.axis_index("reg") * col_width),
    ):
        for low, count in spans(pick.shape[0], TILE):
            shape = (count, rank)
            feature = begin + low + lax.broadcasted_iota(jnp.int32, shape, 0)
            lane = lax.broadcasted_iota(jnp.int32, shape, 1)
            run_start = rank + lane * rank - (lane * (lane - 1)) // 2
            run_end = run_start + rank - lane
            in_run = (feature >= run_start) & (feature < run_end)
            shift = jnp.sum(jnp.where(in_run, run_start - lane, 0), axis=1, keepdims=True)
            pick[low : low + count, :rank] = in_run.astype(jnp.float32).astype(jnp.bfloat16)
            pick[low : low + count, rank:] = (lane == feature - shift).astype(jnp.float32).astype(jnp.bfloat16)


def select(zero, rank, row_width, col_width):
    row_pad, col_pad = round_up(row_width, 16), round_up(col_width + rank, TILE)
    return pl.pallas_call(
        functools.partial(select_kernel, row_width, col_width),
        out_specs=[WHOLE] * 3,
        out_shape=[
            pltpu.VMEM((row_pad, 2 * rank), jnp.bfloat16),
            pltpu.VMEM((col_pad - rank, 2 * rank), jnp.bfloat16),
            pltpu.VMEM(zero.shape, zero.dtype),
        ],
        compiler_params=pltpu.CompilerParams(vmem_limit_bytes=8 * MIB),
        cost_estimate=LONG,
        name="select",
    )()


def feature_rows(first, pick, states):
    rank = pick.shape[1] // 2
    left, right = pick[:, :rank], pick[:, rank:]
    rows = [
        jnp.dot(jnp.concatenate([one_hot, one_hot], axis=1), states, preferred_element_type=jnp.float32)
        for one_hot in (left, right)
    ]
    feature = first + lax.broadcasted_iota(jnp.int32, (pick.shape[0], 1), 0)
    return ((rows[0] + (feature < rank).astype(jnp.float32)) * rows[1]).astype(jnp.bfloat16)


def lay_out(pieces, states, moments):
    rank, at = moments.shape[0], 0
    for piece in pieces:
        for low in range(0, piece.shape[0], 3 * rank):
            columns = slice(at, at + piece.shape[1])
            states[:, columns] = piece[low : low + 2 * rank]
            moments[:, columns] = piece[low + 2 * rank : low + 3 * rank]
            at += piece.shape[1]


def spans(total, most):
    return [(low, min(most, total - low)) for low in range(0, total, most)]


def fill_rows(row_width, pick, states, row_feat, columns):
    first = lax.axis_index("rows") * row_width
    for low, size in spans(row_feat.shape[0], ROWS):
        row_feat[low : low + size, columns] = feature_rows(first + low, pick[low : low + size], states[...])


def fill_columns(col_width, pick, states, moments, col_feat, left, right, columns):
    first, end = lax.axis_index("reg") * col_width, min(right, pick.shape[0])
    col_feat[left:end, columns] = feature_rows(first + left, pick[left:end], states[...])
    if end < right:
        col_feat[end:right, columns] = moments[...]


def prepare_kernel(count, row_width, col_width, *refs):
    pieces, (row_pick, col_pick, row_feat, col_feat, *zero, states, moments) = refs[:count], refs[count:]
    for ref in zero:
        ref[...] = jnp.zeros_like(ref)
    lay_out(pieces, states, moments)
    fill_rows(row_width, row_pick, states, row_feat, slice(None))
    for left, width in spans(col_feat.shape[0], COLS):
        fill_columns(col_width, col_pick, states, moments, col_feat, left, left + width, slice(None))


def prepare(picks, pieces, waiting, cost, rank, row_width, col_width):
    times = sum(piece.size for piece in pieces) // (3 * rank)
    row_pad, col_pad = round_up(row_width, 16), round_up(col_width + rank, TILE)
    return pl.pallas_call(
        functools.partial(prepare_kernel, len(pieces), row_width, col_width),
        in_specs=[WHOLE] * (len(pieces) + 2),
        out_specs=[WHOLE] * (2 + len(waiting)),
        out_shape=[pltpu.VMEM(shape, jnp.bfloat16) for shape in [(row_pad, times), (col_pad, times), *waiting]],
        scratch_shapes=[pltpu.VMEM((n * rank, times), jnp.bfloat16) for n in (2, 1)],
        compiler_params=pltpu.CompilerParams(vmem_limit_bytes=12 * MIB),
        cost_estimate=cost,
        name="prepare",
    )(*map(in_vmem, pieces), *map(in_vmem, picks))


def sum_kernel(count, extra, held, ready, total_time, row_width, col_width, *refs):
    pieces, refs = refs[:count], refs[count:]
    acc_in, refs = (refs[0], refs[1:]) if held else (None, refs)
    (row_ready, col_ready), refs = (refs[:2], refs[2:]) if ready else ((None, None), refs)
    row_pick, col_pick, *refs = refs[extra:]
    states, moments, row_feat, col_feat = refs[-4:]
    rank = moments.shape[0]
    row_pad, col_pad = row_feat.shape[0], col_feat.shape[0]
    columns = slice(row_feat.shape[1] - states.shape[1], row_feat.shape[1])
    before = slice(0, columns.start)
    lay_out(pieces, states, moments)
    fill_rows(row_width, row_pick, states, row_feat, columns)
    if ready:
        row_feat[:, before] = row_ready[...]
    copies = []
    for left, width in spans(col_pad, COLS):
        fill_columns(col_width, col_pick, states, moments, col_feat, left, left + width, columns)
        if ready:
            col_feat[left : left + width, before] = col_ready[left : left + width]
        for low, size in spans(row_pad, ROWS):
            block = lax.dot_general(
                row_feat[low : low + size], col_feat[left : left + width], (((1,), (1,)), ((), ())),
                preferred_element_type=jnp.float32,
            )
            if held:
                block = acc_in[low : low + size, left : left + width] + block
            if total_time is None:
                refs[0][low : low + size, left : left + width] = block
                if left + low == 0:
                    refs[1][...] = jnp.zeros_like(refs[1])
                continue
            gram_hbm, rhs_hbm, gram, rhs, sems = refs[:5]
            block = block * (1 / total_time) if total_time & (total_time - 1) == 0 else block / float(total_time)
            rows = pl.ds(low, min(size, row_width - low))
            if left < col_width:
                part = pl.ds(left, min(width, col_width - left))
                gram[rows, part] = block[: rows.size, : part.size]
                copies.append(pltpu.make_async_copy(gram.at[rows, part], gram_hbm.at[rows, part], sems.at[len(copies)]))
                copies[-1].start()
            if left + width == col_pad:
                rhs[rows] = block[: rows.size, width - rank :]
                copies.append(pltpu.make_async_copy(rhs.at[rows], rhs_hbm.at[rows], sems.at[len(copies)]))
                copies[-1].start()
    for copy in copies:
        copy.wait()


def add_up(picks, place, pieces, held, ready, total_time, waiting, cost, rank, row_width, col_width):
    times = sum(piece.size for piece in pieces) // (3 * rank)
    all_times = times + (ready[0].shape[1] if ready else 0)
    row_pad, col_pad = round_up(row_width, 16), round_up(col_width + rank, TILE)
    operands = [*map(in_vmem, pieces), *map(in_vmem, held), *map(in_vmem, ready), *map(in_vmem, place), *map(in_vmem, picks)]
    scratch = [
        pltpu.VMEM((2 * rank, times), jnp.bfloat16),
        pltpu.VMEM((rank, times), jnp.bfloat16),
        pltpu.VMEM((row_pad, all_times), jnp.bfloat16),
        pltpu.VMEM((col_pad, all_times), jnp.bfloat16),
    ]
    if total_time is None:
        out_specs = [WHOLE, WHOLE]
        out_shape = [pltpu.VMEM((row_pad, col_pad), jnp.float32), pltpu.VMEM(waiting, jnp.bfloat16)]
    else:
        out_specs = [ANYWHERE, ANYWHERE]
        out_shape = [jax.ShapeDtypeStruct((row_width, n), jnp.float32) for n in (col_width, rank)]
        scratch = [
            pltpu.VMEM((row_width, col_width), jnp.float32),
            pltpu.VMEM((row_width, rank), jnp.float32),
            pltpu.SemaphoreType.DMA((len(spans(row_pad, ROWS)) * (len(spans(col_pad, COLS)) + 1),)),
        ] + scratch
    return pl.pallas_call(
        functools.partial(sum_kernel, len(pieces), len(place), bool(held), bool(ready), total_time, row_width, col_width),
        in_specs=[WHOLE] * len(operands),
        out_specs=out_specs,
        out_shape=out_shape,
        scratch_shapes=scratch,
        compiler_params=pltpu.CompilerParams(vmem_limit_bytes=(24 if total_time else 12) * MIB),
        cost_estimate=cost,
        name="add_up_last" if total_time else "add_up",
    )(*operands)


def encode(states, moments):
    coded, exponents = [], []
    for array in (states, lax.reduce_precision(moments, 8, 7)):
        largest = jnp.max(jnp.abs(array), axis=0, keepdims=True)
        exponents.append(jnp.ceil(jnp.log2(jnp.maximum(largest, 1e-37))))
        coded.append(array * jnp.exp2(-exponents[-1]))
    last = lax.broadcasted_iota(jnp.int32, (16, states.shape[1]), 0)
    return jnp.concatenate([*coded, jnp.where(last == 0, *exponents)]).astype(jnp.float16)


def decode(coded, rank):
    coded = coded.astype(jnp.float32)
    states = coded[:rank] * jnp.exp2(coded[2 * rank : 2 * rank + 1])
    moments = coded[rank : 2 * rank] * jnp.exp2(coded[2 * rank + 1 : 2 * rank + 2])
    return split(states, moments)


def split(states, moments):
    high = lax.reduce_precision(states, 8, 7)
    return jnp.concatenate([high, states - high, moments]).astype(jnp.bfloat16)


def per_device(snapshots, rates, basis):
    rank = basis.shape[1]
    width = rank + rank * (rank + 1) // 2
    size_rows, size_reg = lax.axis_size("rows"), lax.axis_size("reg")
    row_width, col_width = width // size_rows, width // size_reg
    total_time = snapshots.shape[1] * size_reg
    shape = (rank, row_width, col_width)

    place = jnp.stack([lax.axis_index("rows") * row_width, lax.axis_index("reg") * col_width]).astype(jnp.int32)
    swap = [(i, i ^ 1) for i in range(size_rows)]
    keep, send = project(basis, snapshots, rates)
    chip = keep + lax.ppermute(send, "rows", swap)
    plane = [[(2 * a + c, 2 * b + c) for a, b in perm for c in range(2)] for perm in partners(size_rows // 2)]
    total = chip
    for perm in plane:
        total = total + lax.ppermute(chip, "rows", perm)
    *picks, zero = select(chip, *shape)
    total = total + zero
    states, moments = total[:rank], total[rank:]
    mine, coded = split(states, moments), encode(states, moments)

    own = [mine, lax.ppermute(mine, "rows", swap)]
    near = lax.ppermute(coded, "reg", [(n, size_reg - 1 - n) for n in range(size_reg)])
    places = [(row, reg) for row in range(size_rows) for reg in range(size_reg)]
    high, low, moments = jnp.split(own[1].astype(jnp.float32), 3)
    whole = jnp.concatenate([coded, encode(high + low, moments)])
    far = []
    for k in range(1, size_reg - 1, 2):
        perm = [(n, row * size_reg + (reg ^ (k + row % 2))) for n, (row, reg) in enumerate(places)]
        far.append(lax.ppermute(whole, ("rows", "reg"), perm))
    *held, zero = add_up(picks, [], own, [], [], None, coded.shape, LONG, *shape)
    near = decode(near + zero.astype(coded.dtype), rank)
    waiting = (len(far) * whole.shape[0], whole.shape[1])
    pieces = [near, lax.ppermute(near, "rows", swap)]
    *held, zero = add_up(picks, [place], pieces, held, [], None, waiting, FREE, *shape)
    far = jnp.concatenate(far) + zero.astype(coded.dtype)
    far = jnp.concatenate([decode(slab, rank) for slab in jnp.split(far, size_reg - 2)])
    other = lax.ppermute(far, "rows", swap)
    ready = prepare(picks, [far], [], FREE, *shape)
    return tuple(add_up(picks, [place], [other], held, ready, total_time, None, FREE, *shape))


def solution(mesh):
    return jax.shard_map(
        per_device,
        mesh=mesh,
        in_specs=(P("rows", "reg"), P("rows", "reg"), P("rows", None)),
        out_specs=(P("rows", "reg"), P("rows", None)),
        check_vma=False,
    )
```

```python
import functools

import jax
import jax.numpy as jnp
from jax import lax
from jax.experimental import pallas as pl
from jax.experimental.pallas import tpu as pltpu
from jax.sharding import PartitionSpec as P

TILE = 256
BLOCK = (528, 1152)
LAST_BLOCK = (352, 768)
CHUNKS = (12,12,12,12,8,4,4)
MIB = 1 << 20


def round_up(value, step):
    return (value + step - 1) // step * step


def partners(size):
    if size & (size - 1) == 0:
        return [[(i, i ^ k) for i in range(size)] for k in range(1, size)]
    return [[(i, (i + k) % size) for i in range(size)] for k in range(1, size)]


WHOLE = pl.BlockSpec(memory_space=pltpu.VMEM)
ANYWHERE = pl.BlockSpec(memory_space=pl.ANY)
LONG = pl.CostEstimate(flops=20_000_000_000, bytes_accessed=0, transcendentals=0)
FREE = pl.CostEstimate(flops=0, bytes_accessed=0, transcendentals=0)


def in_hbm(array):
    return pltpu.with_memory_space_constraint(array, pltpu.HBM)


def in_vmem(array):
    return pltpu.with_memory_space_constraint(array, pltpu.VMEM)


def project_kernel(chunks, basis_hbm, snap_hbm, rate_hbm, keep_ref, send_ref, basis, snap, rate, acc, sems):
    copies = []
    for c, chunk in enumerate(chunks):
        part = pl.ds(*chunk)
        copies.append(
            [
                pltpu.make_async_copy(source.at[part], target.at[part], sems.at[k, c])
                for k, (source, target) in enumerate(((basis_hbm, basis), (snap_hbm, snap), (rate_hbm, rate)))
            ]
        )
        for copy in copies[-1]:
            copy.start()
    for c, chunk in enumerate(chunks):
        for copy in copies[c]:
            copy.wait()
        part = pl.ds(*chunk)
        left = basis[part, :].T
        for k, array in enumerate((snap, rate)):
            product = jnp.dot(left, array[part, :], preferred_element_type=jnp.float32)
            if c == 0:
                acc[k] = product
            else:
                acc[k] += product
    rank, half = acc.shape[1], acc.shape[2] // 2
    core = lax.axis_index("rows") % 2
    mine = pl.multiple_of(core * half, half)
    other = pl.multiple_of(half - core * half, half)
    for k in range(2):
        keep_ref[k * rank : (k + 1) * rank] = acc[k, :, pl.ds(mine, half)]
        send_ref[k * rank : (k + 1) * rank] = acc[k, :, pl.ds(other, half)]


def project(basis, snapshots, rates):
    rows, rank = basis.shape
    times = snapshots.shape[1]
    chunks, unit = [(0, rows)], rows // sum(CHUNKS)
    if unit * sum(CHUNKS) == rows and unit % 16 == 0:
        chunks = [(unit * sum(CHUNKS[:c]), unit * size) for c, size in enumerate(CHUNKS)]
    out = pltpu.VMEM((2 * rank, times // 2), jnp.float32)
    return pl.pallas_call(
        functools.partial(project_kernel, chunks),
        in_specs=[ANYWHERE] * 3,
        out_specs=[WHOLE, WHOLE],
        out_shape=[out, out],
        scratch_shapes=[
            pltpu.VMEM((rows, rank), jnp.bfloat16),
            pltpu.VMEM((rows, times), jnp.bfloat16),
            pltpu.VMEM((rows, times), jnp.bfloat16),
            pltpu.VMEM((2, rank, times), jnp.float32),
            pltpu.SemaphoreType.DMA((3, len(chunks))),
        ],
        compiler_params=pltpu.CompilerParams(vmem_limit_bytes=24 * MIB),
        cost_estimate=pl.CostEstimate(
            flops=4 * rows * rank * times, bytes_accessed=2 * rows * (rank + 2 * times), transcendentals=0
        ),
        name="project",
    )(in_hbm(basis), in_hbm(snapshots), in_hbm(rates))


def select_kernel(row_width, col_width, row_pick, col_pick, zero_ref):
    rank = row_pick.shape[1] // 2
    zero_ref[...] = jnp.zeros_like(zero_ref)
    for pick, begin in (
        (row_pick, lax.axis_index("rows") * row_width),
        (col_pick, lax.axis_index("reg") * col_width),
    ):
        for low, count in spans(pick.shape[0], TILE):
            shape = (count, rank)
            feature = begin + low + lax.broadcasted_iota(jnp.int32, shape, 0)
            lane = lax.broadcasted_iota(jnp.int32, shape, 1)
            run_start = rank + lane * rank - (lane * (lane - 1)) // 2
            run_end = run_start + rank - lane
            in_run = (feature >= run_start) & (feature < run_end)
            shift = jnp.sum(jnp.where(in_run, run_start - lane, 0), axis=1, keepdims=True)
            pick[low : low + count, :rank] = in_run.astype(jnp.float32).astype(jnp.bfloat16)
            pick[low : low + count, rank:] = (lane == feature - shift).astype(jnp.float32).astype(jnp.bfloat16)


def select(zero, rank, row_width, col_width):
    row_pad, col_pad = round_up(row_width, 16), round_up(col_width + rank, TILE)
    return pl.pallas_call(
        functools.partial(select_kernel, row_width, col_width),
        out_specs=[WHOLE] * 3,
        out_shape=[
            pltpu.VMEM((row_pad, 2 * rank), jnp.bfloat16),
            pltpu.VMEM((col_pad - rank, 2 * rank), jnp.bfloat16),
            pltpu.VMEM(zero.shape, zero.dtype),
        ],
        compiler_params=pltpu.CompilerParams(vmem_limit_bytes=8 * MIB),
        cost_estimate=LONG,
        name="select",
    )()


def feature_rows(first, pick, states):
    rank = pick.shape[1] // 2
    left, right = pick[:, :rank], pick[:, rank:]
    rows = [
        jnp.dot(jnp.concatenate([one_hot, one_hot], axis=1), states, preferred_element_type=jnp.float32)
        for one_hot in (left, right)
    ]
    feature = first + lax.broadcasted_iota(jnp.int32, (pick.shape[0], 1), 0)
    return ((rows[0] + (feature < rank).astype(jnp.float32)) * rows[1]).astype(jnp.bfloat16)


def lay_out(pieces, states, moments):
    rank, at = moments.shape[0], 0
    for piece in pieces:
        for low in range(0, piece.shape[0], 3 * rank):
            columns = slice(at, at + piece.shape[1])
            states[:, columns] = piece[low : low + 2 * rank]
            moments[:, columns] = piece[low + 2 * rank : low + 3 * rank]
            at += piece.shape[1]


def spans(total, most):
    return [(low, min(most, total - low)) for low in range(0, total, most)]


def fill_rows(row_width, pick, states, row_feat, columns):
    first = lax.axis_index("rows") * row_width
    for low, size in spans(row_feat.shape[0], BLOCK[0]):
        row_feat[low : low + size, columns] = feature_rows(first + low, pick[low : low + size], states[...])


def fill_columns(col_width, pick, states, moments, col_feat, left, right, columns):
    first, end = lax.axis_index("reg") * col_width, min(right, pick.shape[0])
    if left < end:
        col_feat[left:end, columns] = feature_rows(first + left, pick[left:end], states[...])
    if end < right:
        col_feat[end:right, columns] = moments[...]


def prepare_kernel(count, row_width, col_width, *refs):
    pieces, (row_pick, col_pick, row_feat, col_feat, *zero, states, moments) = refs[:count], refs[count:]
    for ref in zero:
        ref[...] = jnp.zeros_like(ref)
    lay_out(pieces, states, moments)
    fill_rows(row_width, row_pick, states, row_feat, slice(None))
    for left, width in spans(col_feat.shape[0], BLOCK[1]):
        fill_columns(col_width, col_pick, states, moments, col_feat, left, left + width, slice(None))


def prepare(picks, pieces, waiting, cost, rank, row_width, col_width):
    times = sum(piece.size for piece in pieces) // (3 * rank)
    row_pad, col_pad = round_up(row_width, 16), round_up(col_width + rank, TILE)
    return pl.pallas_call(
        functools.partial(prepare_kernel, len(pieces), row_width, col_width),
        in_specs=[WHOLE] * (len(pieces) + 2),
        out_specs=[WHOLE] * (2 + len(waiting)),
        out_shape=[pltpu.VMEM(shape, jnp.bfloat16) for shape in [(row_pad, times), (col_pad, times), *waiting]],
        scratch_shapes=[pltpu.VMEM((n * rank, times), jnp.bfloat16) for n in (2, 1)],
        compiler_params=pltpu.CompilerParams(vmem_limit_bytes=12 * MIB),
        cost_estimate=cost,
        name="prepare",
    )(*map(in_vmem, pieces), *map(in_vmem, picks))


def sum_kernel(count, extra, held, ready, total_time, row_width, col_width, *refs):
    pieces, refs = refs[:count], refs[count:]
    acc_in, refs = (refs[0], refs[1:]) if held else (None, refs)
    (row_ready, col_ready), refs = (refs[:2], refs[2:]) if ready else ((None, None), refs)
    row_pick, col_pick, *refs = refs[extra:]
    states, moments, row_feat, col_feat = refs[-4:]
    rank = moments.shape[0]
    row_pad, col_pad = row_feat.shape[0], col_feat.shape[0]
    columns = slice(row_feat.shape[1] - states.shape[1], row_feat.shape[1])
    before = slice(0, columns.start)
    lay_out(pieces, states, moments)
    fill_rows(row_width, row_pick, states, row_feat, columns)
    if ready:
        row_feat[:, before] = row_ready[...]
    copies, block_size = [], LAST_BLOCK if total_time else BLOCK
    for left, width in spans(col_pad, block_size[1]):
        fill_columns(col_width, col_pick, states, moments, col_feat, left, left + width, columns)
        if ready:
            col_feat[left : left + width, before] = col_ready[left : left + width]
        for low, size in spans(row_pad, block_size[0]):
            block = lax.dot_general(
                row_feat[low : low + size], col_feat[left : left + width], (((1,), (1,)), ((), ())),
                preferred_element_type=jnp.float32,
            )
            if held:
                block = acc_in[low : low + size, left : left + width] + block
            if total_time is None:
                refs[0][low : low + size, left : left + width] = block
                if left + low == 0:
                    refs[1][...] = jnp.zeros_like(refs[1])
                continue
            gram_hbm, rhs_hbm, gram, rhs, sems = refs[:5]
            block = block * (1 / total_time) if total_time & (total_time - 1) == 0 else block / float(total_time)
            rows = pl.ds(low, min(size, row_width - low))
            if left < col_width:
                part = pl.ds(left, min(width, col_width - left))
                gram[rows, part] = block[: rows.size, : part.size]
                copies.append(pltpu.make_async_copy(gram.at[rows, part], gram_hbm.at[rows, part], sems.at[len(copies)]))
                copies[-1].start()
            if left + width == col_pad:
                rhs[rows] = block[: rows.size, width - rank :]
                copies.append(pltpu.make_async_copy(rhs.at[rows], rhs_hbm.at[rows], sems.at[len(copies)]))
                copies[-1].start()
    for copy in copies:
        copy.wait()


def add_up(picks, place, pieces, held, ready, total_time, waiting, cost, rank, row_width, col_width):
    times = sum(piece.size for piece in pieces) // (3 * rank)
    all_times = times + (ready[0].shape[1] if ready else 0)
    row_pad, col_pad = round_up(row_width, 16), round_up(col_width + rank, TILE)
    operands = [*map(in_vmem, pieces), *map(in_vmem, held), *map(in_vmem, ready), *map(in_vmem, place), *map(in_vmem, picks)]
    scratch = [
        pltpu.VMEM((2 * rank, times), jnp.bfloat16),
        pltpu.VMEM((rank, times), jnp.bfloat16),
        pltpu.VMEM((row_pad, all_times), jnp.bfloat16),
        pltpu.VMEM((col_pad, all_times), jnp.bfloat16),
    ]
    if total_time is None:
        out_specs = [WHOLE, WHOLE]
        out_shape = [pltpu.VMEM((row_pad, col_pad), jnp.float32), pltpu.VMEM(waiting, jnp.bfloat16)]
    else:
        out_specs = [ANYWHERE, ANYWHERE]
        out_shape = [jax.ShapeDtypeStruct((row_width, n), jnp.float32) for n in (col_width, rank)]
        scratch = [
            pltpu.VMEM((row_width, col_width), jnp.float32),
            pltpu.VMEM((row_width, rank), jnp.float32),
            pltpu.SemaphoreType.DMA((len(spans(row_pad, LAST_BLOCK[0])) * (len(spans(col_pad, LAST_BLOCK[1])) + 1),)),
        ] + scratch
    return pl.pallas_call(
        functools.partial(sum_kernel, len(pieces), len(place), bool(held), bool(ready), total_time, row_width, col_width),
        in_specs=[WHOLE] * len(operands),
        out_specs=out_specs,
        out_shape=out_shape,
        scratch_shapes=scratch,
        compiler_params=pltpu.CompilerParams(vmem_limit_bytes=(24 if total_time else 12) * MIB),
        cost_estimate=cost,
        name="add_up_last" if total_time else "add_up",
    )(*operands)


def encode(states, moments):
    coded, exponents = [], []
    for array in (states, lax.reduce_precision(moments, 8, 7)):
        largest = jnp.max(jnp.abs(array), axis=0, keepdims=True)
        exponents.append(jnp.ceil(jnp.log2(jnp.maximum(largest, 1e-37))))
        coded.append(array * jnp.exp2(-exponents[-1]))
    last = lax.broadcasted_iota(jnp.int32, (16, states.shape[1]), 0)
    return jnp.concatenate([*coded, jnp.where(last == 0, *exponents)]).astype(jnp.float16)


def decode(coded, rank):
    coded = coded.astype(jnp.float32).reshape(-1, 2 * rank + 16, coded.shape[1])
    states = coded[:, :rank] * jnp.exp2(coded[:, 2 * rank : 2 * rank + 1])
    moments = coded[:, rank : 2 * rank] * jnp.exp2(coded[:, 2 * rank + 1 : 2 * rank + 2])
    return split(states, moments).reshape(-1, coded.shape[2])


def split(states, moments):
    high = lax.reduce_precision(states, 8, 7)
    return jnp.concatenate([high, states - high, moments], axis=-2).astype(jnp.bfloat16)


def per_device(snapshots, rates, basis):
    rank = basis.shape[1]
    width = rank + rank * (rank + 1) // 2
    size_rows, size_reg = lax.axis_size("rows"), lax.axis_size("reg")
    row_width, col_width = width // size_rows, width // size_reg
    total_time = snapshots.shape[1] * size_reg
    shape = (rank, row_width, col_width)

    place = jnp.stack([lax.axis_index("rows") * row_width, lax.axis_index("reg") * col_width]).astype(jnp.int32)
    swap = [(i, i ^ 1) for i in range(size_rows)]
    keep, send = project(basis, snapshots, rates)
    chip = keep + lax.ppermute(send, "rows", swap)
    chips = size_rows // 2
    total = chip
    for k in range(1, chips):
        turned = k ^ 3 if chips % 4 == 0 and k % 4 in (1, 2) else k
        perm = [(n, n ^ 2 * (turned if n % 2 else k)) for n in range(size_rows)]
        total = total + lax.ppermute(chip, "rows", perm)
    *picks, zero = select(chip, *shape)
    total = total + zero
    states, moments = total[:rank], total[rank:]
    mine, coded = split(states, moments), encode(states, moments)

    own = [mine, lax.ppermute(mine, "rows", swap)]
    near = lax.ppermute(coded, "reg", [(n, size_reg - 1 - n) for n in range(size_reg)])
    places = [(row, reg) for row in range(size_rows) for reg in range(size_reg)]
    high, low, moments = jnp.split(own[1].astype(jnp.float32), 3)
    whole = jnp.concatenate([coded, encode(high + low, moments)])
    far = []
    for k in range(1, size_reg - 1, 2):
        perm = [(n, row * size_reg + (reg ^ (k + row % 2))) for n, (row, reg) in enumerate(places)]
        far.append(lax.ppermute(whole, ("rows", "reg"), perm))
    *held, zero = add_up(picks, [], own, [], [], None, coded.shape, LONG, *shape)
    near = near + zero.astype(coded.dtype)
    waiting = (len(far) * whole.shape[0], whole.shape[1])
    pieces = [decode(piece, rank) for piece in (near, lax.ppermute(near, "rows", swap))]
    *held, zero = add_up(picks, [place], pieces, held, [], None, waiting, FREE, *shape)
    far = jnp.concatenate(far) + zero.astype(coded.dtype)
    other = decode(lax.ppermute(far, "rows", swap), rank)
    ready = prepare(picks, [decode(far, rank)], [], FREE, *shape)
    return tuple(add_up(picks, [place], [other], held, ready, total_time, None, FREE, *shape))


def solution(mesh):
    return jax.shard_map(
        per_device,
        mesh=mesh,
        in_specs=(P("rows", "reg"), P("rows", "reg"), P("rows", None)),
        out_specs=(P("rows", "reg"), P("rows", None)),
        check_vma=False,
    )
```

```python
import functools

import jax
import jax.numpy as jnp
from jax import lax
from jax.experimental import pallas as pl
from jax.experimental.pallas import tpu as pltpu
from jax.sharding import PartitionSpec as P

TILE = 256
BLOCK = (528, 2304)
LAST_BLOCK = (352, 768)
CHUNKS = (12,12,12,12,8,4,4)
MIB = 1 << 20


def round_up(value, step):
    return (value + step - 1) // step * step


def partners(size):
    if size & (size - 1) == 0:
        return [[(i, i ^ k) for i in range(size)] for k in range(1, size)]
    return [[(i, (i + k) % size) for i in range(size)] for k in range(1, size)]


WHOLE = pl.BlockSpec(memory_space=pltpu.VMEM)
ANYWHERE = pl.BlockSpec(memory_space=pl.ANY)
LONG = pl.CostEstimate(flops=20_000_000_000, bytes_accessed=0, transcendentals=0)
FREE = pl.CostEstimate(flops=0, bytes_accessed=0, transcendentals=0)


def in_hbm(array):
    return pltpu.with_memory_space_constraint(array, pltpu.HBM)


def in_vmem(array):
    return pltpu.with_memory_space_constraint(array, pltpu.VMEM)


def project_kernel(chunks, basis_hbm, snap_hbm, rate_hbm, keep_ref, send_ref, basis, snap, rate, acc, sems):
    copies = []
    for c, chunk in enumerate(chunks):
        part = pl.ds(*chunk)
        copies.append(
            [
                pltpu.make_async_copy(source.at[part], target.at[part], sems.at[k, c])
                for k, (source, target) in enumerate(((basis_hbm, basis), (snap_hbm, snap), (rate_hbm, rate)))
            ]
        )
        for copy in copies[-1]:
            copy.start()
    for c, chunk in enumerate(chunks):
        for copy in copies[c]:
            copy.wait()
        part = pl.ds(*chunk)
        left = basis[part, :].T
        for k, array in enumerate((snap, rate)):
            product = jnp.dot(left, array[part, :], preferred_element_type=jnp.float32)
            if c == 0:
                acc[k] = product
            else:
                acc[k] += product
    rank, half = acc.shape[1], acc.shape[2] // 2
    core = lax.axis_index("rows") % 2
    mine = pl.multiple_of(core * half, half)
    other = pl.multiple_of(half - core * half, half)
    for k in range(2):
        keep_ref[k * rank : (k + 1) * rank] = acc[k, :, pl.ds(mine, half)]
        send_ref[k * rank : (k + 1) * rank] = acc[k, :, pl.ds(other, half)]


def project(basis, snapshots, rates):
    rows, rank = basis.shape
    times = snapshots.shape[1]
    chunks, unit = [(0, rows)], rows // sum(CHUNKS)
    if unit * sum(CHUNKS) == rows and unit % 16 == 0:
        chunks = [(unit * sum(CHUNKS[:c]), unit * size) for c, size in enumerate(CHUNKS)]
    out = pltpu.VMEM((2 * rank, times // 2), jnp.float32)
    return pl.pallas_call(
        functools.partial(project_kernel, chunks),
        in_specs=[ANYWHERE] * 3,
        out_specs=[WHOLE, WHOLE],
        out_shape=[out, out],
        scratch_shapes=[
            pltpu.VMEM((rows, rank), jnp.bfloat16),
            pltpu.VMEM((rows, times), jnp.bfloat16),
            pltpu.VMEM((rows, times), jnp.bfloat16),
            pltpu.VMEM((2, rank, times), jnp.float32),
            pltpu.SemaphoreType.DMA((3, len(chunks))),
        ],
        compiler_params=pltpu.CompilerParams(vmem_limit_bytes=24 * MIB),
        cost_estimate=pl.CostEstimate(
            flops=4 * rows * rank * times, bytes_accessed=2 * rows * (rank + 2 * times), transcendentals=0
        ),
        name="project",
    )(in_hbm(basis), in_hbm(snapshots), in_hbm(rates))


def select_kernel(row_width, col_width, row_pick, col_pick, zero_ref):
    rank = row_pick.shape[1] // 2
    zero_ref[...] = jnp.zeros_like(zero_ref)
    for pick, begin in (
        (row_pick, lax.axis_index("rows") * row_width),
        (col_pick, lax.axis_index("reg") * col_width),
    ):
        for low, count in spans(pick.shape[0], TILE):
            shape = (count, rank)
            feature = begin + low + lax.broadcasted_iota(jnp.int32, shape, 0)
            lane = lax.broadcasted_iota(jnp.int32, shape, 1)
            run_start = rank + lane * rank - (lane * (lane - 1)) // 2
            run_end = run_start + rank - lane
            in_run = (feature >= run_start) & (feature < run_end)
            shift = jnp.sum(jnp.where(in_run, run_start - lane, 0), axis=1, keepdims=True)
            pick[low : low + count, :rank] = in_run.astype(jnp.float32).astype(jnp.bfloat16)
            pick[low : low + count, rank:] = (lane == feature - shift).astype(jnp.float32).astype(jnp.bfloat16)


def select(zero, rank, row_width, col_width):
    row_pad, col_pad = round_up(row_width, 16), round_up(col_width + rank, TILE)
    return pl.pallas_call(
        functools.partial(select_kernel, row_width, col_width),
        out_specs=[WHOLE] * 3,
        out_shape=[
            pltpu.VMEM((row_pad, 2 * rank), jnp.bfloat16),
            pltpu.VMEM((col_pad - rank, 2 * rank), jnp.bfloat16),
            pltpu.VMEM(zero.shape, zero.dtype),
        ],
        compiler_params=pltpu.CompilerParams(vmem_limit_bytes=8 * MIB),
        cost_estimate=LONG,
        name="select",
    )()


def feature_rows(first, pick, states):
    rank = pick.shape[1] // 2
    left, right = pick[:, :rank], pick[:, rank:]
    rows = [
        jnp.dot(jnp.concatenate([one_hot, one_hot], axis=1), states, preferred_element_type=jnp.float32)
        for one_hot in (left, right)
    ]
    feature = first + lax.broadcasted_iota(jnp.int32, (pick.shape[0], 1), 0)
    return ((rows[0] + (feature < rank).astype(jnp.float32)) * rows[1]).astype(jnp.bfloat16)


def lay_out(pieces, states, moments):
    rank, at = moments.shape[0], 0
    for piece in pieces:
        for low in range(0, piece.shape[0], 3 * rank):
            columns = slice(at, at + piece.shape[1])
            states[:, columns] = piece[low : low + 2 * rank]
            moments[:, columns] = piece[low + 2 * rank : low + 3 * rank]
            at += piece.shape[1]


def spans(total, most):
    return [(low, min(most, total - low)) for low in range(0, total, most)]


def fill_rows(row_width, pick, states, row_feat, columns):
    first = lax.axis_index("rows") * row_width
    for low, size in spans(row_feat.shape[0], BLOCK[0]):
        row_feat[low : low + size, columns] = feature_rows(first + low, pick[low : low + size], states[...])


def fill_columns(col_width, pick, states, moments, col_feat, left, right, columns):
    first, end = lax.axis_index("reg") * col_width, min(right, pick.shape[0])
    if left < end:
        col_feat[left:end, columns] = feature_rows(first + left, pick[left:end], states[...])
    if end < right:
        col_feat[end:right, columns] = moments[...]


def prepare_kernel(count, row_width, col_width, *refs):
    pieces, (row_pick, col_pick, row_feat, col_feat, *zero, states, moments) = refs[:count], refs[count:]
    for ref in zero:
        ref[...] = jnp.zeros_like(ref)
    lay_out(pieces, states, moments)
    fill_rows(row_width, row_pick, states, row_feat, slice(None))
    for left, width in spans(col_feat.shape[0], BLOCK[1]):
        fill_columns(col_width, col_pick, states, moments, col_feat, left, left + width, slice(None))


def prepare(picks, pieces, waiting, cost, rank, row_width, col_width):
    times = sum(piece.size for piece in pieces) // (3 * rank)
    row_pad, col_pad = round_up(row_width, 16), round_up(col_width + rank, TILE)
    return pl.pallas_call(
        functools.partial(prepare_kernel, len(pieces), row_width, col_width),
        in_specs=[WHOLE] * (len(pieces) + 2),
        out_specs=[WHOLE] * (2 + len(waiting)),
        out_shape=[pltpu.VMEM(shape, jnp.bfloat16) for shape in [(row_pad, times), (col_pad, times), *waiting]],
        scratch_shapes=[pltpu.VMEM((n * rank, times), jnp.bfloat16) for n in (2, 1)],
        compiler_params=pltpu.CompilerParams(vmem_limit_bytes=12 * MIB),
        cost_estimate=cost,
        name="prepare",
    )(*map(in_vmem, pieces), *map(in_vmem, picks))


def sum_kernel(count, extra, held, ready, total_time, row_width, col_width, *refs):
    pieces, refs = refs[:count], refs[count:]
    acc_in, refs = (refs[0], refs[1:]) if held else (None, refs)
    (row_ready, col_ready), refs = (refs[:2], refs[2:]) if ready else ((None, None), refs)
    row_pick, col_pick, *refs = refs[extra:]
    states, moments, row_feat, col_feat = refs[-4:]
    rank = moments.shape[0]
    row_pad, col_pad = row_feat.shape[0], col_feat.shape[0]
    columns = slice(row_feat.shape[1] - states.shape[1], row_feat.shape[1])
    before = slice(0, columns.start)
    lay_out(pieces, states, moments)
    fill_rows(row_width, row_pick, states, row_feat, columns)
    if ready:
        row_feat[:, before] = row_ready[...]
    copies, block_size = [], LAST_BLOCK if total_time else BLOCK
    for left, width in spans(col_pad, block_size[1]):
        fill_columns(col_width, col_pick, states, moments, col_feat, left, left + width, columns)
        if ready:
            col_feat[left : left + width, before] = col_ready[left : left + width]
        for low, size in spans(row_pad, block_size[0]):
            block = lax.dot_general(
                row_feat[low : low + size], col_feat[left : left + width], (((1,), (1,)), ((), ())),
                preferred_element_type=jnp.float32,
            )
            if held:
                block = acc_in[low : low + size, left : left + width] + block
            if total_time is None:
                refs[0][low : low + size, left : left + width] = block
                if left + low == 0:
                    refs[1][...] = jnp.zeros_like(refs[1])
                continue
            gram_hbm, rhs_hbm, gram, rhs, sems = refs[:5]
            block = block * (1 / total_time) if total_time & (total_time - 1) == 0 else block / float(total_time)
            rows = pl.ds(low, min(size, row_width - low))
            if left < col_width:
                part = pl.ds(left, min(width, col_width - left))
                gram[rows, part] = block[: rows.size, : part.size]
                copies.append(pltpu.make_async_copy(gram.at[rows, part], gram_hbm.at[rows, part], sems.at[len(copies)]))
                copies[-1].start()
            if left + width == col_pad:
                rhs[rows] = block[: rows.size, width - rank :]
                copies.append(pltpu.make_async_copy(rhs.at[rows], rhs_hbm.at[rows], sems.at[len(copies)]))
                copies[-1].start()
    for copy in copies:
        copy.wait()


def add_up(picks, place, pieces, held, ready, total_time, waiting, cost, rank, row_width, col_width):
    times = sum(piece.size for piece in pieces) // (3 * rank)
    all_times = times + (ready[0].shape[1] if ready else 0)
    row_pad, col_pad = round_up(row_width, 16), round_up(col_width + rank, TILE)
    operands = [*map(in_vmem, pieces), *map(in_vmem, held), *map(in_vmem, ready), *map(in_vmem, place), *map(in_vmem, picks)]
    scratch = [
        pltpu.VMEM((2 * rank, times), jnp.bfloat16),
        pltpu.VMEM((rank, times), jnp.bfloat16),
        pltpu.VMEM((row_pad, all_times), jnp.bfloat16),
        pltpu.VMEM((col_pad, all_times), jnp.bfloat16),
    ]
    if total_time is None:
        out_specs = [WHOLE, WHOLE]
        out_shape = [pltpu.VMEM((row_pad, col_pad), jnp.float32), pltpu.VMEM(waiting, jnp.bfloat16)]
    else:
        out_specs = [ANYWHERE, ANYWHERE]
        out_shape = [jax.ShapeDtypeStruct((row_width, n), jnp.float32) for n in (col_width, rank)]
        scratch = [
            pltpu.VMEM((row_width, col_width), jnp.float32),
            pltpu.VMEM((row_width, rank), jnp.float32),
            pltpu.SemaphoreType.DMA((len(spans(row_pad, LAST_BLOCK[0])) * (len(spans(col_pad, LAST_BLOCK[1])) + 1),)),
        ] + scratch
    return pl.pallas_call(
        functools.partial(sum_kernel, len(pieces), len(place), bool(held), bool(ready), total_time, row_width, col_width),
        in_specs=[WHOLE] * len(operands),
        out_specs=out_specs,
        out_shape=out_shape,
        scratch_shapes=scratch,
        compiler_params=pltpu.CompilerParams(vmem_limit_bytes=(24 if total_time else 12) * MIB),
        cost_estimate=cost,
        name="add_up_last" if total_time else "add_up",
    )(*operands)


def encode(states, moments):
    coded, exponents = [], []
    for array in (states, lax.reduce_precision(moments, 8, 7)):
        largest = jnp.max(jnp.abs(array), axis=0, keepdims=True)
        exponents.append(jnp.ceil(jnp.log2(jnp.maximum(largest, 1e-37))))
        coded.append(array * jnp.exp2(-exponents[-1]))
    last = lax.broadcasted_iota(jnp.int32, (16, states.shape[1]), 0)
    return jnp.concatenate([*coded, jnp.where(last == 0, *exponents)]).astype(jnp.float16)


def decode(coded, rank):
    coded = coded.astype(jnp.float32).reshape(-1, 2 * rank + 16, coded.shape[1])
    states = coded[:, :rank] * jnp.exp2(coded[:, 2 * rank : 2 * rank + 1])
    moments = coded[:, rank : 2 * rank] * jnp.exp2(coded[:, 2 * rank + 1 : 2 * rank + 2])
    return split(states, moments).reshape(-1, coded.shape[2])


def split(states, moments):
    high = lax.reduce_precision(states, 8, 7)
    return jnp.concatenate([high, states - high, moments], axis=-2).astype(jnp.bfloat16)


def per_device(snapshots, rates, basis):
    rank = basis.shape[1]
    width = rank + rank * (rank + 1) // 2
    size_rows, size_reg = lax.axis_size("rows"), lax.axis_size("reg")
    row_width, col_width = width // size_rows, width // size_reg
    total_time = snapshots.shape[1] * size_reg
    shape = (rank, row_width, col_width)

    place = jnp.stack([lax.axis_index("rows") * row_width, lax.axis_index("reg") * col_width]).astype(jnp.int32)
    swap = [(i, i ^ 1) for i in range(size_rows)]
    keep, send = project(basis, snapshots, rates)
    chip = keep + lax.ppermute(send, "rows", swap)
    chips = size_rows // 2
    total = chip
    for k in range(1, chips):
        turned = k ^ 3 if chips % 4 == 0 and k % 4 in (1, 2) else k
        perm = [(n, n ^ 2 * (turned if n % 2 else k)) for n in range(size_rows)]
        total = total + lax.ppermute(chip, "rows", perm)
    *picks, zero = select(chip, *shape)
    total = total + zero
    states, moments = total[:rank], total[rank:]
    mine, coded = split(states, moments), encode(states, moments)

    own = [mine, lax.ppermute(mine, "rows", swap)]
    near = lax.ppermute(coded, "reg", [(n, size_reg - 1 - n) for n in range(size_reg)])
    places = [(row, reg) for row in range(size_rows) for reg in range(size_reg)]
    high, low, moments = jnp.split(own[1].astype(jnp.float32), 3)
    whole = jnp.concatenate([coded, encode(high + low, moments)])
    far = []
    for k in range(1, size_reg - 1, 2):
        perm = [(n, row * size_reg + (reg ^ (k + row % 2))) for n, (row, reg) in enumerate(places)]
        far.append(lax.ppermute(whole, ("rows", "reg"), perm))
    *held, zero = add_up(picks, [], own, [], [], None, coded.shape, LONG, *shape)
    near = near + zero.astype(coded.dtype)
    waiting = (len(far) * whole.shape[0], whole.shape[1])
    pieces = [decode(piece, rank) for piece in (near, lax.ppermute(near, "rows", swap))]
    *held, zero = add_up(picks, [place], pieces, held, [], None, waiting, FREE, *shape)
    far = jnp.concatenate(far) + zero.astype(coded.dtype)
    other = decode(lax.ppermute(far, "rows", swap), rank)
    ready = prepare(picks, [decode(far, rank)], [], FREE, *shape)
    return tuple(add_up(picks, [place], [other], held, ready, total_time, None, FREE, *shape))


def solution(mesh):
    return jax.shard_map(
        per_device,
        mesh=mesh,
        in_specs=(P("rows", "reg"), P("rows", "reg"), P("rows", None)),
        out_specs=(P("rows", "reg"), P("rows", None)),
        check_vma=False,
    )
```

```python
import functools

import jax
import jax.numpy as jnp
from jax import lax
from jax.experimental import pallas as pl
from jax.experimental.pallas import tpu as pltpu
from jax.sharding import PartitionSpec as P

TILE = 256
BLOCK = (528, 2304)
LAST_BLOCK = (352, 768)
CHUNKS = (12,12,12,12,8,4,4)
MIB = 1 << 20


def round_up(value, step):
    return (value + step - 1) // step * step


def partners(size):
    if size & (size - 1) == 0:
        return [[(i, i ^ k) for i in range(size)] for k in range(1, size)]
    return [[(i, (i + k) % size) for i in range(size)] for k in range(1, size)]


WHOLE = pl.BlockSpec(memory_space=pltpu.VMEM)
ANYWHERE = pl.BlockSpec(memory_space=pl.ANY)
LONG = pl.CostEstimate(flops=20_000_000_000, bytes_accessed=0, transcendentals=0)
FREE = pl.CostEstimate(flops=0, bytes_accessed=0, transcendentals=0)


def in_hbm(array):
    return pltpu.with_memory_space_constraint(array, pltpu.HBM)


def in_vmem(array):
    return pltpu.with_memory_space_constraint(array, pltpu.VMEM)


def project_kernel(chunks, basis_hbm, snap_hbm, rate_hbm, keep_ref, send_ref, basis, snap, rate, acc, sems):
    copies = []
    for c, chunk in enumerate(chunks):
        part = pl.ds(*chunk)
        copies.append(
            [
                pltpu.make_async_copy(source.at[part], target.at[part], sems.at[k, c])
                for k, (source, target) in enumerate(((basis_hbm, basis), (snap_hbm, snap), (rate_hbm, rate)))
            ]
        )
        for copy in copies[-1]:
            copy.start()
    for c, chunk in enumerate(chunks):
        for copy in copies[c]:
            copy.wait()
        part = pl.ds(*chunk)
        left = basis[part, :].T
        for k, array in enumerate((snap, rate)):
            product = jnp.dot(left, array[part, :], preferred_element_type=jnp.float32)
            if c == 0:
                acc[k] = product
            else:
                acc[k] += product
    rank, half = acc.shape[1], acc.shape[2] // 2
    core = lax.axis_index("rows") % 2
    mine = pl.multiple_of(core * half, half)
    other = pl.multiple_of(half - core * half, half)
    for k in range(2):
        keep_ref[k * rank : (k + 1) * rank] = acc[k, :, pl.ds(mine, half)]
        send_ref[k * rank : (k + 1) * rank] = acc[k, :, pl.ds(other, half)]


def project(basis, snapshots, rates):
    rows, rank = basis.shape
    times = snapshots.shape[1]
    chunks, unit = [(0, rows)], rows // sum(CHUNKS)
    if unit * sum(CHUNKS) == rows and unit % 16 == 0:
        chunks = [(unit * sum(CHUNKS[:c]), unit * size) for c, size in enumerate(CHUNKS)]
    out = pltpu.VMEM((2 * rank, times // 2), jnp.float32)
    return pl.pallas_call(
        functools.partial(project_kernel, chunks),
        in_specs=[ANYWHERE] * 3,
        out_specs=[WHOLE, WHOLE],
        out_shape=[out, out],
        scratch_shapes=[
            pltpu.VMEM((rows, rank), jnp.bfloat16),
            pltpu.VMEM((rows, times), jnp.bfloat16),
            pltpu.VMEM((rows, times), jnp.bfloat16),
            pltpu.VMEM((2, rank, times), jnp.float32),
            pltpu.SemaphoreType.DMA((3, len(chunks))),
        ],
        compiler_params=pltpu.CompilerParams(vmem_limit_bytes=24 * MIB),
        cost_estimate=pl.CostEstimate(
            flops=4 * rows * rank * times, bytes_accessed=2 * rows * (rank + 2 * times), transcendentals=0
        ),
        name="project",
    )(in_hbm(basis), in_hbm(snapshots), in_hbm(rates))


def select_kernel(row_width, col_width, row_pick, col_pick, zero_ref):
    rank = row_pick.shape[1] // 2
    zero_ref[...] = jnp.zeros_like(zero_ref)
    for pick, begin in (
        (row_pick, lax.axis_index("rows") * row_width),
        (col_pick, lax.axis_index("reg") * col_width),
    ):
        for low, count in spans(pick.shape[0], TILE):
            shape = (count, rank)
            feature = begin + low + lax.broadcasted_iota(jnp.int32, shape, 0)
            lane = lax.broadcasted_iota(jnp.int32, shape, 1)
            run_start = rank + lane * rank - (lane * (lane - 1)) // 2
            run_end = run_start + rank - lane
            in_run = (feature >= run_start) & (feature < run_end)
            shift = jnp.sum(jnp.where(in_run, run_start - lane, 0), axis=1, keepdims=True)
            pick[low : low + count, :rank] = in_run.astype(jnp.float32).astype(jnp.bfloat16)
            pick[low : low + count, rank:] = (lane == feature - shift).astype(jnp.float32).astype(jnp.bfloat16)


def select(zero, rank, row_width, col_width):
    row_pad, col_pad = round_up(row_width, 16), round_up(col_width + rank, TILE)
    return pl.pallas_call(
        functools.partial(select_kernel, row_width, col_width),
        out_specs=[WHOLE] * 3,
        out_shape=[
            pltpu.VMEM((row_pad, 2 * rank), jnp.bfloat16),
            pltpu.VMEM((col_pad - rank, 2 * rank), jnp.bfloat16),
            pltpu.VMEM(zero.shape, zero.dtype),
        ],
        compiler_params=pltpu.CompilerParams(vmem_limit_bytes=8 * MIB),
        cost_estimate=LONG,
        name="select",
    )()


def feature_rows(first, pick, states):
    rank = pick.shape[1] // 2
    left, right = pick[:, :rank], pick[:, rank:]
    rows = [
        jnp.dot(jnp.concatenate([one_hot, one_hot], axis=1), states, preferred_element_type=jnp.float32)
        for one_hot in (left, right)
    ]
    feature = first + lax.broadcasted_iota(jnp.int32, (pick.shape[0], 1), 0)
    return ((rows[0] + (feature < rank).astype(jnp.float32)) * rows[1]).astype(jnp.bfloat16)


def lay_out(pieces, states, moments):
    rank, at = moments.shape[0], 0
    for piece in pieces:
        for low in range(0, piece.shape[0], 3 * rank):
            columns = slice(at, at + piece.shape[1])
            states[:, columns] = piece[low : low + 2 * rank]
            moments[:, columns] = piece[low + 2 * rank : low + 3 * rank]
            at += piece.shape[1]


def spans(total, most):
    return [(low, min(most, total - low)) for low in range(0, total, most)]


def fill_rows(row_width, pick, states, row_feat, columns):
    first = lax.axis_index("rows") * row_width
    for low, size in spans(row_feat.shape[0], BLOCK[0]):
        row_feat[low : low + size, columns] = feature_rows(first + low, pick[low : low + size], states[...])


def fill_columns(col_width, pick, states, moments, col_feat, left, right, columns):
    first, end = lax.axis_index("reg") * col_width, min(right, pick.shape[0])
    if left < end:
        col_feat[left:end, columns] = feature_rows(first + left, pick[left:end], states[...])
    if end < right:
        col_feat[end:right, columns] = moments[...]


def prepare_kernel(count, row_width, col_width, *refs):
    pieces, (row_pick, col_pick, row_feat, col_feat, *zero, states, moments) = refs[:count], refs[count:]
    for ref in zero:
        ref[...] = jnp.zeros_like(ref)
    lay_out(pieces, states, moments)
    fill_rows(row_width, row_pick, states, row_feat, slice(None))
    for left, width in spans(col_feat.shape[0], BLOCK[1]):
        fill_columns(col_width, col_pick, states, moments, col_feat, left, left + width, slice(None))


def prepare(picks, pieces, waiting, cost, rank, row_width, col_width):
    times = sum(piece.size for piece in pieces) // (3 * rank)
    row_pad, col_pad = round_up(row_width, 16), round_up(col_width + rank, TILE)
    return pl.pallas_call(
        functools.partial(prepare_kernel, len(pieces), row_width, col_width),
        in_specs=[WHOLE] * (len(pieces) + 2),
        out_specs=[WHOLE] * (2 + len(waiting)),
        out_shape=[pltpu.VMEM(shape, jnp.bfloat16) for shape in [(row_pad, times), (col_pad, times), *waiting]],
        scratch_shapes=[pltpu.VMEM((n * rank, times), jnp.bfloat16) for n in (2, 1)],
        compiler_params=pltpu.CompilerParams(vmem_limit_bytes=12 * MIB),
        cost_estimate=cost,
        name="prepare",
    )(*map(in_vmem, pieces), *map(in_vmem, picks))


def sum_kernel(count, extra, held, ready, total_time, row_width, col_width, *refs):
    pieces, refs = refs[:count], refs[count:]
    acc_in, refs = (refs[0], refs[1:]) if held else (None, refs)
    (row_ready, col_ready), refs = (refs[:2], refs[2:]) if ready else ((None, None), refs)
    row_pick, col_pick, *refs = refs[extra:]
    states, moments, row_feat, col_feat = refs[-4:]
    rank = moments.shape[0]
    row_pad, col_pad = row_feat.shape[0], col_feat.shape[0]
    columns = slice(row_feat.shape[1] - states.shape[1], row_feat.shape[1])
    before = slice(0, columns.start)
    lay_out(pieces, states, moments)
    fill_rows(row_width, row_pick, states, row_feat, columns)
    if ready:
        row_feat[:, before] = row_ready[...]
    copies, block_size = [], LAST_BLOCK if total_time else BLOCK
    for left, width in spans(col_pad, block_size[1]):
        fill_columns(col_width, col_pick, states, moments, col_feat, left, left + width, columns)
        if ready:
            col_feat[left : left + width, before] = col_ready[left : left + width]
        for low, size in spans(row_pad, block_size[0]):
            block = lax.dot_general(
                row_feat[low : low + size], col_feat[left : left + width], (((1,), (1,)), ((), ())),
                preferred_element_type=jnp.float32,
            )
            if held:
                block = acc_in[low : low + size, left : left + width] + block
            if total_time is None:
                refs[0][low : low + size, left : left + width] = block
                if left + low == 0:
                    refs[1][...] = jnp.zeros_like(refs[1])
                continue
            gram_hbm, rhs_hbm, gram, rhs, sems = refs[:5]
            block = block * (1 / total_time) if total_time & (total_time - 1) == 0 else block / float(total_time)
            rows = pl.ds(low, min(size, row_width - low))
            if left < col_width:
                part = pl.ds(left, min(width, col_width - left))
                gram[rows, part] = block[: rows.size, : part.size]
                copies.append(pltpu.make_async_copy(gram.at[rows, part], gram_hbm.at[rows, part], sems.at[len(copies)]))
                copies[-1].start()
            if left + width == col_pad:
                rhs[rows] = block[: rows.size, width - rank :]
                copies.append(pltpu.make_async_copy(rhs.at[rows], rhs_hbm.at[rows], sems.at[len(copies)]))
                copies[-1].start()
    for copy in copies:
        copy.wait()


def add_up(picks, place, pieces, held, ready, total_time, waiting, cost, rank, row_width, col_width):
    times = sum(piece.size for piece in pieces) // (3 * rank)
    all_times = times + (ready[0].shape[1] if ready else 0)
    row_pad, col_pad = round_up(row_width, 16), round_up(col_width + rank, TILE)
    operands = [*map(in_vmem, pieces), *map(in_vmem, held), *map(in_vmem, ready), *map(in_vmem, place), *map(in_vmem, picks)]
    scratch = [
        pltpu.VMEM((2 * rank, times), jnp.bfloat16),
        pltpu.VMEM((rank, times), jnp.bfloat16),
        pltpu.VMEM((row_pad, all_times), jnp.bfloat16),
        pltpu.VMEM((col_pad, all_times), jnp.bfloat16),
    ]
    if total_time is None:
        out_specs = [WHOLE, WHOLE]
        out_shape = [pltpu.VMEM((row_pad, col_pad), jnp.float32), pltpu.VMEM(waiting, jnp.bfloat16)]
    else:
        out_specs = [ANYWHERE, ANYWHERE]
        out_shape = [jax.ShapeDtypeStruct((row_width, n), jnp.float32) for n in (col_width, rank)]
        scratch = [
            pltpu.VMEM((row_width, col_width), jnp.float32),
            pltpu.VMEM((row_width, rank), jnp.float32),
            pltpu.SemaphoreType.DMA((len(spans(row_pad, LAST_BLOCK[0])) * (len(spans(col_pad, LAST_BLOCK[1])) + 1),)),
        ] + scratch
    return pl.pallas_call(
        functools.partial(sum_kernel, len(pieces), len(place), bool(held), bool(ready), total_time, row_width, col_width),
        in_specs=[WHOLE] * len(operands),
        out_specs=out_specs,
        out_shape=out_shape,
        scratch_shapes=scratch,
        compiler_params=pltpu.CompilerParams(vmem_limit_bytes=(24 if total_time else 12) * MIB),
        cost_estimate=cost,
        name="add_up_last" if total_time else "add_up",
    )(*operands)


def encode(states, moments):
    coded, exponents = [], []
    for array in (states, lax.reduce_precision(moments, 8, 7)):
        largest = jnp.max(jnp.abs(array), axis=0, keepdims=True)
        exponents.append(jnp.ceil(jnp.log2(jnp.maximum(largest, 1e-37))))
        coded.append(array * jnp.exp2(-exponents[-1]))
    last = lax.broadcasted_iota(jnp.int32, (16, states.shape[1]), 0)
    return jnp.concatenate([*coded, jnp.where(last == 0, *exponents)]).astype(jnp.float16)


def decode(coded, rank):
    coded = coded.astype(jnp.float32).reshape(-1, 2 * rank + 16, coded.shape[1])
    states = coded[:, :rank] * jnp.exp2(coded[:, 2 * rank : 2 * rank + 1])
    moments = coded[:, rank : 2 * rank] * jnp.exp2(coded[:, 2 * rank + 1 : 2 * rank + 2])
    return split(states, moments).reshape(-1, coded.shape[2])


def split(states, moments):
    high = lax.reduce_precision(states, 8, 7)
    return jnp.concatenate([high, states - high, moments], axis=-2).astype(jnp.bfloat16)


def per_device(snapshots, rates, basis):
    rank = basis.shape[1]
    width = rank + rank * (rank + 1) // 2
    size_rows, size_reg = lax.axis_size("rows"), lax.axis_size("reg")
    row_width, col_width = width // size_rows, width // size_reg
    total_time = snapshots.shape[1] * size_reg
    shape = (rank, row_width, col_width)

    place = jnp.stack([lax.axis_index("rows") * row_width, lax.axis_index("reg") * col_width]).astype(jnp.int32)
    swap = [(i, i ^ 1) for i in range(size_rows)]
    keep, send = project(basis, snapshots, rates)
    chip = keep + lax.ppermute(send, "rows", swap)
    chips = size_rows // 2
    total = chip
    for k in sorted(range(1, chips), key=lambda k: (k % 2, k)):
        turned = k ^ 3 if chips % 4 == 0 and k % 4 in (1, 2) else k
        perm = [(n, n ^ 2 * (turned if n % 2 else k)) for n in range(size_rows)]
        total = total + lax.ppermute(chip, "rows", perm)
    *picks, zero = select(chip, *shape)
    total = total + zero
    states, moments = total[:rank], total[rank:]
    mine, coded = split(states, moments), encode(states, moments)

    own = [mine, lax.ppermute(mine, "rows", swap)]
    near = lax.ppermute(coded, "reg", [(n, size_reg - 1 - n) for n in range(size_reg)])
    places = [(row, reg) for row in range(size_rows) for reg in range(size_reg)]
    high, low, moments = jnp.split(own[1].astype(jnp.float32), 3)
    whole = jnp.concatenate([coded, encode(high + low, moments)])
    far = []
    for k in range(1, size_reg - 1, 2):
        perm = [(n, row * size_reg + (reg ^ (k + row % 2))) for n, (row, reg) in enumerate(places)]
        far.append(lax.ppermute(whole, ("rows", "reg"), perm))
    *held, zero = add_up(picks, [], own, [], [], None, coded.shape, LONG, *shape)
    near = near + zero.astype(coded.dtype)
    waiting = (len(far) * whole.shape[0], whole.shape[1])
    pieces = [decode(piece, rank) for piece in (near, lax.ppermute(near, "rows", swap))]
    *held, zero = add_up(picks, [place], pieces, held, [], None, waiting, FREE, *shape)
    far = jnp.concatenate(far) + zero.astype(coded.dtype)
    other = decode(lax.ppermute(far, "rows", swap), rank)
    ready = prepare(picks, [decode(far, rank)], [], FREE, *shape)
    return tuple(add_up(picks, [place], [other], held, ready, total_time, None, FREE, *shape))


def solution(mesh):
    return jax.shard_map(
        per_device,
        mesh=mesh,
        in_specs=(P("rows", "reg"), P("rows", "reg"), P("rows", None)),
        out_specs=(P("rows", "reg"), P("rows", None)),
        check_vma=False,
    )
```
